256 devices in a mesh: ctx: 32 (over y_hi, z, core), tp: 8 (over x, y_lo).
Axes of the slice: x: 4, y: 4 (y_hi: 2, y_lo: 2; y = y_hi * 2 + y_lo), z: 8, core: 2. Of those that a mesh axis runs over, the one named last changes fastest.
Arguments:
- tokens: bfloat16 [8192, 5120], P('ctx', 'tp'), may hold values from -65 to 65
- tangent: bfloat16 [8192, 5120], P('ctx', 'tp'), may hold values from -6 to 6
- modulation: bfloat16 [3, 5120], P(None, 'tp'), may hold values from -3 to 3
- mod_tangent: bfloat16 [3, 5120], P(None, 'tp'), may hold values from -3 to 3
- up_weight: bfloat16 [5120, 6912], P('ctx', 'tp'), may hold values from -0.078125 to 0.078125
- down_weight: bfloat16 [6912, 5120], P('tp', 'ctx'), may hold values from -0.125 to 0.125
Outputs:
- block_out: bfloat16 [8192, 5120], P('ctx', 'tp')
- block_tangent: bfloat16 [8192, 5120], P('ctx', 'tp')
The draws below stay inside these ranges and needn't reach their ends.
All inputs are finite; a program needn't handle non-finite values.
Results may differ from the reference program's by a relative error of at most 0.019.
Values may be sent and summed in bfloat16 or wider, within the bound.
No kernel may reach another device: no remote copies, remote signals or barrier semaphores. Data moves between devices by JAX's collectives and lax.ppermute only.
A program may use at most 64 MiB of HBM per device.

```python
import math
import jax
import jax.numpy as jnp
from jax import lax

D = 5120
FF = 6912
TOKENS = 8192
FF_DEV = 864
N_TP = 8


def draw_tokens(key, part):
    key = jax.random.fold_in(key, 11)
    key_rows, key_cols, key_base = jax.random.split(key, 3)
    row_scale = jnp.exp(jax.random.uniform(key_rows, (TOKENS, 1), jnp.float32, math.log(0.3), math.log(3.0)))
    position = jnp.arange(D, dtype=jnp.float32)[None, :] / (D - 1)
    ramp_scale = jnp.exp(math.log(0.6) + position * (math.log(1.8) - math.log(0.6)))
    col_scale = jnp.exp(jax.random.uniform(key_cols, (1, D), jnp.float32, math.log(0.3), math.log(3.0))) * ramp_scale
    base_values = jax.random.truncated_normal(key_base, -4.0, 4.0, (TOKENS, D), jnp.float32)
    return (base_values * row_scale * col_scale).astype(jnp.bfloat16)


def raised(drawn, rng, source, target, parts, factor):
    owner, partner = [(jnp.arange(drawn.shape[dim]) // (drawn.shape[dim] // parts)).reshape([-1 if axis == dim else 1 for axis in range(drawn.ndim)]) for dim in (source, target)]
    chosen = jax.random.permutation(rng, parts)[partner]
    strong = (owner == chosen) | (owner == (partner + parts // 2) % parts)
    return jnp.where(strong, factor * drawn, drawn)


def level_of(own_key, extent, pieces, low, largest):
    factor_of = 1.0
    for dim, blocks in pieces:
        heights = jax.random.uniform(jax.random.fold_in(jax.random.fold_in(own_key, 6), dim), (blocks,), jnp.float32, low / len(pieces), largest / len(pieces))
        factor_of = factor_of * jnp.repeat(jnp.exp(heights), extent[dim] // blocks).reshape((-1,) + (1,) * (len(extent) - 1 - dim))
    return factor_of


def bell_draw(rng, dims, scale, bound, cuts=(), kind=jnp.bfloat16):
    entries = jax.random.normal(rng, dims, jnp.float32) * scale
    if len(cuts) > 0:
        entries = level_of(rng, dims, cuts, -0.22, 0.18) * entries
    return jnp.clip(entries, min=-bound, max=bound).astype(kind)


def bell_draw_with(key, dims, scale, reach, cuts, heavy, kind=jnp.bfloat16):
    entries = scale * jax.random.normal(key, dims, jnp.float32)
    if cuts:
        entries = entries * level_of(key, dims, cuts, -0.22, 0.18)
    return jnp.clip(raised(entries, jax.random.fold_in(key, 3), *heavy), -reach, reach).astype(kind)


def setup_inputs(seed: int = 0) -> dict:
    splits = jax.random.split(jax.random.key(seed), 7)
    tokens = draw_tokens(jax.random.fold_in(splits[6], 71), 0)
    tangent = bell_draw(splits[1], (TOKENS, D), 1.0, 6.0, ((0, 32), (1, 8)))
    modulation = bell_draw(splits[2], (3, D), 0.5, 3.0, ((1, 8),))
    mod_tangent = bell_draw(splits[3], (3, D), 0.5, 3.0, ((1, 8),))
    up_weight = bell_draw(splits[4], (D, FF), D ** -0.5, 0.078125, ((0, 32), (1, 8)))
    down_weight = bell_draw_with(splits[5], (FF, D), FF ** -0.5, 0.125, ((0, 8), (1, 32)), (0, 1, 32, 2.75))
    return dict(tokens=tokens, tangent=tangent, modulation=modulation, mod_tangent=mod_tangent, up_weight=up_weight, down_weight=down_weight)


def shape_rows(primal, tan_rows, moment_sums, modulation, mod_tangent):
    row_mean = moment_sums[0][:, None] / D
    row_square = moment_sums[1][:, None] / D
    inverse_std = lax.rsqrt(row_square - row_mean * row_mean + 1e-06)
    tan_mean = moment_sums[2][:, None] / D
    crossed = (moment_sums[3][:, None] / D - row_mean * tan_mean) * inverse_std
    normed = (primal - row_mean) * inverse_std
    tnormed = (tan_rows - tan_mean) * inverse_std - normed * crossed * inverse_std
    mod_now = modulation.astype(jnp.float32)
    mod_tan = mod_tangent.astype(jnp.float32)
    inputs = normed * (1.0 + mod_now[1]) + mod_now[0]
    tinputs = tnormed * (1.0 + mod_now[1]) + normed * mod_tan[1] + mod_tan[0]
    return jnp.concatenate([inputs, tinputs], 0).astype(jnp.bfloat16)

def activate(up_pre, row_count):
    up_now = up_pre[:row_count]
    up_tan = up_pre[row_count:]
    coeff = math.sqrt(2.0 / math.pi)
    th = jnp.tanh(coeff * (up_now + 0.044715 * up_now * up_now * up_now))
    active = 0.5 * up_now * (1.0 + th)
    slopes = 0.5 * (1.0 + th) + 0.5 * up_now * (1.0 - th * th) * coeff * (1.0 + 3.0 * 0.044715 * up_now * up_now)
    return jnp.concatenate([active, slopes * up_tan], 0).astype(jnp.bfloat16)

def reference(tokens, tangent, modulation, mod_tangent, up_weight, down_weight):
    primal = tokens.astype(jnp.float32)
    tan_rows = tangent.astype(jnp.float32)
    moment_sums = jnp.stack([lax.optimization_barrier(jnp.sum(primal, axis=1)), lax.optimization_barrier(jnp.sum(primal * primal, axis=1)), lax.optimization_barrier(jnp.sum(tan_rows, axis=1)), lax.optimization_barrier(jnp.sum(primal * tan_rows, axis=1))])
    both_rows = shape_rows(primal, tan_rows, moment_sums, modulation, mod_tangent)
    up_pre = jnp.dot(both_rows, up_weight, preferred_element_type=jnp.float32)
    hidden = activate(up_pre, TOKENS)

    def add_block(running, block_index):
        block_start = (block_index * FF_DEV).astype(jnp.int32)
        hidden_block = lax.dynamic_slice_in_dim(hidden, block_start, FF_DEV, 1)
        weight_block = lax.dynamic_slice_in_dim(down_weight, block_start, FF_DEV, 0)
        partial_out = jnp.dot(hidden_block, weight_block, preferred_element_type=jnp.float32).astype(jnp.bfloat16)
        partial_out = lax.optimization_barrier(partial_out)
        return (running + partial_out.astype(jnp.float32), None)
    mixed_all, unused = lax.scan(add_block, jnp.zeros((2 * TOKENS, D), jnp.float32), jnp.arange(N_TP, dtype=jnp.int32))
    mixed = mixed_all[:TOKENS]
    tmixed = mixed_all[TOKENS:]
    mod_now = modulation.astype(jnp.float32)
    mod_tan = mod_tangent.astype(jnp.float32)
    block_out = (mod_now[2] * mixed).astype(jnp.bfloat16)
    block_tangent = (mod_tan[2] * mixed + mod_now[2] * tmixed).astype(jnp.bfloat16)
    return (block_out, block_tangent)
```

```python
import functools
import math

import jax
import jax.numpy as jnp
from jax import lax
from jax.experimental import pallas as pl
from jax.experimental.pallas import tpu as pltpu
from jax.sharding import PartitionSpec as P

D = 5120
ROWS = 256
COLS = 640
FF = 864
WBLK = 160
HALF = 80
VMEM_LIMIT = 56 * 1024 * 1024


def ctx_perm(move):
    pairs = []
    for i in range(32):
        h, z, c = move(i // 16, (i // 2) % 8, i % 2)
        pairs.append((i, ((h % 2) * 8 + z % 8) * 2 + c % 2))
    return pairs


def tp_perm(move):
    pairs = []
    for i in range(8):
        x, y = move(i // 2, i % 2)
        pairs.append((i, (x % 4) * 2 + y % 2))
    return pairs


def x_up(v):
    return lax.ppermute(v, "tp", tp_perm(lambda x, y: (x + 1, y)))


def x_down(v):
    return lax.ppermute(v, "tp", tp_perm(lambda x, y: (x - 1, y)))


def y_near(v):
    return lax.ppermute(v, "tp", tp_perm(lambda x, y: (x, y + 1)))


def y_far(v):
    return lax.ppermute(v, "ctx", ctx_perm(lambda h, z, c: (h + 1, z, c)))


def core_swap(v):
    return lax.ppermute(v, "ctx", ctx_perm(lambda h, z, c: (h, z, c + 1)))


def z_ring(v):
    return lax.ppermute(v, "ctx", ctx_perm(lambda h, z, c: (h, z + 1 - 2 * c, c)))


def place():
    t = lax.axis_index("tp")
    i = lax.axis_index("ctx")
    return t // 2, t % 2, i // 16, (i // 2) % 8, i % 2


def near_order(x, y, h, z):
    owner = h * 4 + z // 2
    dx = (owner // 2 - x + 4) % 4
    dy = (owner % 2 - y + 2) % 2
    side = jnp.where(dx == 3, 2, 3) + 2 * dy
    return jnp.where(dx == 0, dy, jnp.where(dx == 2, 6 + dy, side))


def gather_weights(blocks):
    mine = jnp.concatenate([blocks, core_swap(blocks)], 0)
    first = z_ring(mine)
    second = z_ring(first)
    third = z_ring(second)
    fourth = z_ring(third[:2])
    return [
        mine,
        first,
        core_swap(first),
        second,
        core_swap(second),
        third,
        core_swap(third),
        fourth,
        core_swap(fourth),
    ]


def piece_slots(height):
    x, y, h, z, c = place()
    out = []
    for array in range(9):
        step = (array + 1) // 2
        swapped = array > 0 and array % 2 == 0
        sign = 1 - 2 * c
        there = (z + (step * sign if swapped else -step * sign) + 8) % 8
        lead = 1 - c if swapped else c
        for block in range(2 if array >= 7 else 4):
            core = lead if block < 2 else 1 - lead
            side = h if block % 2 == 0 else 1 - h
            spot = near_order(x, y, side, there) * 4 + (there % 2) * 2 + core
            out.append((array, block, spot * height))
    return out


def shape_kernel(*refs):
    toks, tans, mods, out = refs[:8], refs[8:16], refs[16:24], refs[24]
    tok = [r[...].astype(jnp.float32) for r in toks]
    tan = [r[...].astype(jnp.float32) for r in tans]

    def total(parts):
        return sum(jnp.sum(p, axis=1, keepdims=True) for p in parts)

    row_mean = total(tok) / D
    row_square = total([t * t for t in tok]) / D
    inverse_std = lax.rsqrt(row_square - row_mean * row_mean + 1e-06)
    tan_mean = total(tan) / D
    crossed = (total([t * u for t, u in zip(tok, tan)]) / D - row_mean * tan_mean) * inverse_std
    for k in range(8):
        mod = mods[k][...].astype(jnp.float32)
        normed = (tok[k] - row_mean) * inverse_std
        tnormed = (tan[k] - tan_mean) * inverse_std - normed * crossed * inverse_std
        gain = 1.0 + mod[1:2]
        inputs = normed * gain + mod[0:1]
        tinputs = tnormed * gain + normed * mod[4:5] + mod[3:4]
        cols = pl.ds(k * COLS, COLS)
        out[0, :, cols] = inputs.astype(jnp.bfloat16)
        out[1, :, cols] = tinputs.astype(jnp.bfloat16)


def shape_rows(whole, split):
    tile = 32
    steps = ROWS // tile

    def rows(first):
        return pl.BlockSpec((tile, COLS), lambda i, first=first: (i + first, 0))

    def tail(index):
        return pl.BlockSpec((16, COLS), lambda i, index=index: (index, 0))

    toks = list(whole) + [s[0] for s in split]
    rest = list(whole) + [s[1] for s in split]
    specs = [rows(0)] * 8 + [rows(steps)] * 6 + [rows(0)] * 2 + [tail(32)] * 6 + [tail(16)] * 2
    return pl.pallas_call(
        shape_kernel,
        grid=(steps,),
        in_specs=specs,
        out_specs=pl.BlockSpec((2, tile, D), lambda i: (0, i, 0)),
        out_shape=jax.ShapeDtypeStruct((2, ROWS, D), jnp.bfloat16),
        compiler_params=pltpu.CompilerParams(vmem_limit_bytes=VMEM_LIMIT),
        cost_estimate=pl.CostEstimate(flops=30 * ROWS * D, bytes_accessed=8 * ROWS * D, transcendentals=0),
        name="shape_rows",
    )(*toks, *rest, *rest)


def up_kernel(*refs):
    rows, arrays, out = refs[0], refs[1:10], refs[10]
    rows_v, weight_v, total, sems = refs[11:]
    copies = [pltpu.make_async_copy(rows, rows_v, sems.at[0])]
    for n, (array, block, first) in enumerate(piece_slots(WBLK)):
        target = weight_v.at[pl.ds(pl.multiple_of(first, 32), WBLK), :]
        copies.append(pltpu.make_async_copy(arrays[array].at[block], target, sems.at[n + 1]))
    for copy in copies:
        copy.start()
    for copy in copies:
        copy.wait()
    total[...] = jnp.zeros_like(total)

    def add(k, carry):
        cols = pl.ds(pl.multiple_of(k * COLS, 128), COLS)
        total[...] += jnp.dot(rows_v[:, cols], weight_v[cols, :], preferred_element_type=jnp.float32)
        return carry

    lax.fori_loop(0, 8, add, 0)
    coeff = math.sqrt(2.0 / math.pi)
    tile = 64

    def activate(k, carry):
        now = pl.ds(pl.multiple_of(k * tile, tile), tile)
        later = pl.ds(pl.multiple_of(ROWS + k * tile, tile), tile)
        up = total[now, :]
        square = up * up
        th = jnp.tanh(coeff * (up + 0.044715 * up * square))
        half = 0.5 * (1.0 + th)
        slopes = half + 0.5 * up * (1.0 - th * th) * coeff * (1.0 + 3.0 * 0.044715 * square)
        total[later, :] = slopes * total[later, :]
        total[now, :] = up * half
        return carry

    lax.fori_loop(0, ROWS // tile, activate, 0)
    for k in range(0, FF, 128):
        width = min(128, FF - k)
        out[pl.ds(k, width), :] = total[:, pl.ds(k, width)].T.astype(jnp.bfloat16)


def up_product(rows, arrays):
    return pl.pallas_call(
        up_kernel,
        in_specs=[pl.BlockSpec(memory_space=pl.ANY)] * 10,
        out_specs=pl.BlockSpec(memory_space=pltpu.VMEM),
        out_shape=jax.ShapeDtypeStruct((FF, 2 * ROWS), jnp.bfloat16),
        scratch_shapes=[
            pltpu.VMEM((2 * ROWS, D), jnp.bfloat16),
            pltpu.VMEM((D, FF), jnp.bfloat16),
            pltpu.VMEM((2 * ROWS, FF), jnp.float32),
            pltpu.SemaphoreType.DMA((33,)),
        ],
        compiler_params=pltpu.CompilerParams(vmem_limit_bytes=VMEM_LIMIT),
        cost_estimate=pl.CostEstimate(flops=4 * ROWS * D * FF, bytes_accessed=15000000, transcendentals=ROWS * FF),
        name="up_product",
    )(rows, *arrays)


def down_kernel(*refs):
    hidden, arrays, outs = refs[0], refs[1:10], refs[10:18]
    weight_v, sems = refs[18:]
    copies = []
    for n, (array, block, first) in enumerate(piece_slots(HALF)):
        target = weight_v.at[pl.ds(pl.multiple_of(first, 16), HALF), :]
        copies.append(pltpu.make_async_copy(arrays[array].at[block], target, sems.at[n]))
    for copy in copies:
        copy.start()
    for copy in copies:
        copy.wait()
    for k in (6, 7, 2, 5, 3, 4, 1, 0):
        part = jnp.dot(weight_v[pl.ds(k * 4 * HALF, 4 * HALF), :], hidden[...], preferred_element_type=jnp.float32)
        outs[k][...] = part.astype(jnp.bfloat16)


def down_product(hidden, arrays):
    return pl.pallas_call(
        down_kernel,
        in_specs=[pl.BlockSpec(memory_space=pltpu.VMEM)] + [pl.BlockSpec(memory_space=pl.ANY)] * 9,
        out_specs=[pl.BlockSpec(memory_space=pltpu.VMEM)] * 8,
        out_shape=[jax.ShapeDtypeStruct((4 * HALF, 2 * ROWS), jnp.bfloat16)] * 8,
        scratch_shapes=[
            pltpu.VMEM((32 * HALF, FF), jnp.bfloat16),
            pltpu.SemaphoreType.DMA((32,)),
        ],
        compiler_params=pltpu.CompilerParams(vmem_limit_bytes=VMEM_LIMIT),
        cost_estimate=pl.CostEstimate(flops=2 * ROWS * D * FF, bytes_accessed=8000000, transcendentals=0),
        name="down_product",
    )(hidden, *arrays)


def both(a, b):
    return (a.astype(jnp.float32) + b.astype(jnp.float32)).astype(jnp.bfloat16)


def sum_parts(parts):
    low = x_up(parts[6])
    high = x_down(parts[7])
    from_up = x_down(parts[2])
    partner_a = x_up(parts[5])
    partner_b = x_down(both(parts[4], high))
    from_down = x_up(both(parts[3], low))
    partner = (
        parts[1].astype(jnp.float32) + partner_a.astype(jnp.float32) + partner_b.astype(jnp.float32)
    ).astype(jnp.bfloat16)
    return [parts[0], from_up, from_down, y_near(partner)]


def out_kernel(*refs):
    terms, mod, tmod, block_out, block_tangent, total = refs[:8], refs[8], refs[9], refs[10], refs[11], refs[12]
    for half in range(2):
        for block in range(4):
            source = pl.ds(block * HALF, HALF)
            value = terms[half * 4][source, :].astype(jnp.float32)
            for k in range(1, 4):
                value += terms[half * 4 + k][source, :].astype(jnp.float32)
            total[pl.ds(block * WBLK + half * HALF, HALF), :] = value
    outgate = mod[...].astype(jnp.float32)[2:3]
    toutgate = tmod[...].astype(jnp.float32)[2:3]
    for k in range(0, COLS, 128):
        cols = pl.ds(k, 128)
        tile = total[cols, :].T
        mixed = tile[:ROWS]
        gate = outgate[:, k : k + 128]
        tgate = toutgate[:, k : k + 128]
        block_out[:, cols] = (gate * mixed).astype(jnp.bfloat16)
        block_tangent[:, cols] = (tgate * mixed + gate * tile[ROWS:]).astype(jnp.bfloat16)


def gated(terms, modulation, mod_tangent):
    return pl.pallas_call(
        out_kernel,
        in_specs=[pl.BlockSpec(memory_space=pltpu.VMEM)] * 10,
        out_specs=[pl.BlockSpec(memory_space=pltpu.VMEM)] * 2,
        out_shape=[jax.ShapeDtypeStruct((ROWS, COLS), jnp.bfloat16)] * 2,
        scratch_shapes=[pltpu.VMEM((COLS, 2 * ROWS), jnp.float32)],
        compiler_params=pltpu.CompilerParams(vmem_limit_bytes=VMEM_LIMIT),
        cost_estimate=pl.CostEstimate(flops=10 * ROWS * COLS, bytes_accessed=3500000, transcendentals=0),
        name="gated",
    )(*terms, modulation, mod_tangent)


def shards(tokens, tangent, modulation, mod_tangent, up_weight, down_weight):
    pad = jnp.zeros((10, COLS), jnp.bfloat16)
    own = jnp.concatenate([tokens, tangent, modulation, mod_tangent, pad], 0)
    down_rows = down_weight.T

    ups = jnp.stack([up_weight, y_far(up_weight)])
    downs = jnp.stack([down_rows, y_far(down_rows)])

    near = y_near(own)
    from_low = x_up(own)
    from_high = x_down(own)
    near_low = x_up(near)
    near_high = x_down(near)
    across = (x_up(from_low[:ROWS]), x_down(from_high[ROWS:]))
    near_across = (x_up(near_low[:ROWS]), x_down(near_high[ROWS:]))

    up_arrays = gather_weights(ups)
    down_first = gather_weights(downs[:, :HALF])
    down_second = gather_weights(downs[:, HALF:])

    rows = shape_rows([own, near, from_low, from_high, near_low, near_high], [across, near_across])
    hidden = up_product(rows.reshape(2 * ROWS, D), up_arrays)
    terms = sum_parts(down_product(hidden, down_first)) + sum_parts(down_product(hidden, down_second))
    block_out, block_tangent = gated(terms, modulation, mod_tangent)
    return (block_out, block_tangent)


def solution(mesh):
    return jax.shard_map(
        shards,
        mesh=mesh,
        in_specs=(
            P("ctx", "tp"),
            P("ctx", "tp"),
            P(None, "tp"),
            P(None, "tp"),
            P("ctx", "tp"),
            P("tp", "ctx"),
        ),
        out_specs=(P("ctx", "tp"), P("ctx", "tp")),
        check_vma=False,
    )
```

```python
import functools
import math

import jax
import jax.numpy as jnp
from jax import lax
from jax.experimental import pallas as pl
from jax.experimental.pallas import tpu as pltpu
from jax.sharding import PartitionSpec as P

D = 5120
ROWS = 256
COLS = 640
FF = 864
WBLK = 160
VMEM_LIMIT = 56 * 1024 * 1024


def ctx_perm(move):
    pairs = []
    for i in range(32):
        h, z, c = move(i // 16, (i // 2) % 8, i % 2)
        pairs.append((i, ((h % 2) * 8 + z % 8) * 2 + c % 2))
    return pairs


def tp_perm(move):
    pairs = []
    for i in range(8):
        x, y = move(i // 2, i % 2)
        pairs.append((i, (x % 4) * 2 + y % 2))
    return pairs


def x_up(v):
    return lax.ppermute(v, "tp", tp_perm(lambda x, y: (x + 1, y)))


def x_down(v):
    return lax.ppermute(v, "tp", tp_perm(lambda x, y: (x - 1, y)))


def y_near(v):
    return lax.ppermute(v, "tp", tp_perm(lambda x, y: (x, y + 1)))


def y_far(v):
    return lax.ppermute(v, "ctx", ctx_perm(lambda h, z, c: (h + 1, z, c)))


def core_swap(v):
    return lax.ppermute(v, "ctx", ctx_perm(lambda h, z, c: (h, z, c + 1)))


def z_ring(v):
    return lax.ppermute(v, "ctx", ctx_perm(lambda h, z, c: (h, z + 1 - 2 * c, c)))


def place():
    t = lax.axis_index("tp")
    i = lax.axis_index("ctx")
    return t // 2, t % 2, i // 16, (i // 2) % 8, i % 2


def near_order(x, y, h, z):
    owner = h * 4 + z // 2
    dx = (owner // 2 - x + 4) % 4
    dy = (owner % 2 - y + 2) % 2
    side = jnp.where(dx == 3, 2, 3) + 2 * dy
    return jnp.where(dx == 0, dy, jnp.where(dx == 2, 6 + dy, side))


def after(value, *others):
    return lax.optimization_barrier((value, *others))[0]


def fence(*values):
    return lax.optimization_barrier(values)


START = tuple(((1, 0, 0, own), (0, 0, 0, own)) for own in (1, 0))
FAR_START = tuple(((0, 1, 0, own),) for own in (1, 0))


def ring_step(step):
    blocks = ((0, 0, step, 0), (1, 0, step, 0), (1, 0, step, 1), (0, 0, step, 1))
    if step > 1:
        blocks += ((0, 1, step - 1, 1), (0, 1, step - 1, 0))
    return blocks


RING = {k: ring_step(k) for k in (1, 2, 3)}
RING[4] = ((1, 0, 4, 1), (0, 0, 4, 1), (0, 1, 3, 1), (0, 1, 3, 0))
RING[5] = ((0, 1, 4, 1),)
SIDE = {k: ((1, 1, k, 0), (1, 1, k, 1)) for k in (1, 2, 3)}
SIDE[1] = ((1, 1, 0, 1), *SIDE[1])
SIDE[4] = ((1, 1, 4, 1),)


def ring_blocks(kind, sources, swaps):
    x, y, h, z, c = place()
    out = []
    arrays = [(blocks, False) for blocks in sources]
    for blocks in swaps:
        arrays += [(blocks, False), (blocks, True)]
    for array, (blocks, swapped) in enumerate(arrays):
        for block, (of, stream, step, own) in enumerate(blocks):
            if of != kind:
                continue
            sign = 1 - 2 * c
            there = (z + (step * sign if swapped else -step * sign) + 8) % 8
            core = c if bool(own) != swapped else 1 - c
            spot = near_order(x, y, 1 - h if stream else h, there) * 4 + (there % 2) * 2 + core
            out.append((array, block, stream, spot, there // 2))
    return out


def pack_kernel(tokens, tangent, modulation, mod_tangent, out):
    out[:ROWS, :] = tokens[...]
    out[ROWS : 2 * ROWS, :] = tangent[...]
    mods = [modulation[...].astype(jnp.float32), mod_tangent[...].astype(jnp.float32)]
    tail = jnp.concatenate([*mods, jnp.zeros((10, COLS), jnp.float32)], 0)
    out[2 * ROWS :, :] = tail.astype(jnp.bfloat16)


def packed(*arrays):
    return pl.pallas_call(
        pack_kernel,
        in_specs=[pl.BlockSpec(memory_space=pltpu.VMEM)] * 4,
        out_specs=pl.BlockSpec(memory_space=pltpu.VMEM),
        out_shape=jax.ShapeDtypeStruct((2 * ROWS + 16, COLS), jnp.bfloat16),
        cost_estimate=pl.CostEstimate(flops=0, bytes_accessed=1400000, transcendentals=0),
        name="packed",
    )(*arrays)


def shape_kernel(*refs):
    whole, across_low, across_high, out = refs[:6], refs[6], refs[7], refs[8]
    toks = [(r, 0) for r in whole] + [(across_low, 0), (across_low, ROWS)]
    tans = [(r, ROWS) for r in whole] + [(across_high, 0), (across_high, ROWS + 16)]
    lanes = [(k, pl.ds(n, 128), k * COLS + n) for k in range(8) for n in range(0, COLS, 128)]
    tile = out.shape[1]
    start = pl.program_id(0) * tile

    def load(source, k, cols, first):
        ref, base = source[k]
        return ref[pl.ds(pl.multiple_of(base + first, 16), 16), cols].astype(jnp.float32)

    def sixteen(i, carry):
        first = start + i * 16
        sums = [jnp.zeros((16, 128), jnp.float32) for _ in range(4)]
        for k, cols, _ in lanes:
            t = load(toks, k, cols, first)
            u = load(tans, k, cols, first)
            sums = [sums[0] + t, sums[1] + t * t, sums[2] + u, sums[3] + t * u]
        row_sum, square_sum, tan_sum, cross_sum = [jnp.sum(p, axis=1, keepdims=True) for p in sums]
        row_mean = row_sum / D
        inverse_std = lax.rsqrt(square_sum / D - row_mean * row_mean + 1e-06)
        tan_mean = tan_sum / D
        crossed = (cross_sum / D - row_mean * tan_mean) * inverse_std
        back = crossed * inverse_std
        rows = pl.ds(pl.multiple_of(i * 16, 16), 16)
        for k, cols, place_of in lanes:
            ref, base = tans[k]
            mod = ref[pl.ds(base + ROWS, 16), cols].astype(jnp.float32)
            gain = 1.0 + mod[1:2]
            normed = (load(toks, k, cols, first) - row_mean) * inverse_std
            tnormed = (load(tans, k, cols, first) - tan_mean) * inverse_std - normed * back
            target = pl.ds(place_of, 128)
            out[0, rows, target] = (normed * gain + mod[0:1]).astype(jnp.bfloat16)
            out[1, rows, target] = (tnormed * gain + normed * mod[4:5] + mod[3:4]).astype(jnp.bfloat16)
        return carry

    lax.fori_loop(0, tile // 16, sixteen, 0)


def shape_rows(whole, across_low, across_high):
    tile = 64
    sources = [*whole, across_low, across_high]
    return pl.pallas_call(
        shape_kernel,
        grid=(ROWS // tile,),
        in_specs=[pl.BlockSpec(a.shape, lambda i: (0, 0)) for a in sources],
        out_specs=pl.BlockSpec((2, tile, D), lambda i: (0, i, 0)),
        out_shape=jax.ShapeDtypeStruct((2, ROWS, D), jnp.bfloat16),
        compiler_params=pltpu.CompilerParams(vmem_limit_bytes=VMEM_LIMIT),
        cost_estimate=pl.CostEstimate(flops=30 * ROWS * D, bytes_accessed=8 * ROWS * D, transcendentals=0),
        name="shape_rows",
    )(*sources)


def add_blocks(rows, arrays, blocks, wanted, rows_v, weight_v, total, row_sems, weight_sems, fresh):
    x, y, h, _, _ = place()
    order = [near_order(x, y, 1 - h if stream else h, 2 * pair) for stream, pair in wanted]

    def row_copy(k):
        cols = pl.ds(pl.multiple_of(k * COLS, 128), COLS)
        return pltpu.make_async_copy(rows.at[:, cols], rows_v.at[:, cols], row_sems.at[k])

    for k in order:
        row_copy(k).start()
    for array, block, stream, spot, pair in blocks:
        target = weight_v.at[pl.ds(pl.multiple_of(spot * WBLK, 32), WBLK), :]
        copy = pltpu.make_async_copy(arrays[array].at[block], target, weight_sems.at[spot // 4])
        here = [pair == other for of, other in wanted if of == stream]
        pl.when(functools.reduce(lambda p, q: p | q, here))(copy.start)
    for n, k in enumerate(order):
        cols = pl.ds(pl.multiple_of(k * COLS, 128), COLS)
        row_copy(k).wait()
        block = weight_v.at[cols, :]
        pltpu.make_async_copy(block, block, weight_sems.at[k]).wait()
        part = jnp.dot(rows_v[:, cols], weight_v[cols, :], preferred_element_type=jnp.float32)
        total[...] = part if fresh and n == 0 else total[...] + part


def pair_order():
    z = place()[3]
    side = 2 * (z % 2) - 1
    return [z // 2, (z // 2 + side + 4) % 4, (z // 2 - side + 4) % 4, (z // 2 + 2) % 4]


def up_first_kernel(rows, *refs):
    arrays, total, scratch = refs[:10], refs[10], refs[11:]
    p = pair_order()
    wanted = [(0, p[0]), (0, p[1]), (1, p[0]), (0, p[2]), (1, p[1])]
    add_blocks(rows, arrays, ring_blocks(0, START + FAR_START, [RING[k] for k in (1, 2, 3)]), wanted, *scratch[:2], total, *scratch[2:], True)


def up_second_kernel(rows, before, *refs):
    arrays, out, total, scratch = refs[:6], refs[6], refs[7], refs[8:]
    total[...] = before[...]
    p = pair_order()
    wanted = [(1, p[2]), (0, p[3]), (1, p[3])]
    add_blocks(rows, arrays, ring_blocks(0, (), [RING[k] for k in (3, 4, 5)]), wanted, *scratch[:2], total, *scratch[2:], False)
    coeff = math.sqrt(2.0 / math.pi)
    tile = 16

    def activate(k, carry):
        now = pl.ds(pl.multiple_of(k * tile, tile), tile)
        later = pl.ds(pl.multiple_of(ROWS + k * tile, tile), tile)
        up = total[now, :]
        square = up * up
        th = jnp.tanh(coeff * (up + 0.044715 * up * square))
        half = 0.5 * (1.0 + th)
        slopes = half + 0.5 * up * (1.0 - th * th) * coeff * (1.0 + 3.0 * 0.044715 * square)
        total[later, :] = slopes * total[later, :]
        total[now, :] = up * half
        return carry

    lax.fori_loop(0, ROWS // tile, activate, 0)
    for k in range(0, FF, 128):
        width = min(128, FF - k)
        out[pl.ds(k, width), :] = total[:, pl.ds(k, width)].T.astype(jnp.bfloat16)


UP_SCRATCH = (
    pltpu.VMEM((2 * ROWS, D), jnp.bfloat16),
    pltpu.VMEM((D, FF), jnp.bfloat16),
    pltpu.SemaphoreType.DMA((8,)),
    pltpu.SemaphoreType.DMA((8,)),
)


def up_first(rows, arrays):
    return pl.pallas_call(
        up_first_kernel,
        in_specs=[pl.BlockSpec(memory_space=pl.ANY)] * 11,
        out_specs=pl.BlockSpec(memory_space=pltpu.VMEM),
        out_shape=jax.ShapeDtypeStruct((2 * ROWS, FF), jnp.float32),
        scratch_shapes=UP_SCRATCH,
        compiler_params=pltpu.CompilerParams(vmem_limit_bytes=VMEM_LIMIT),
        cost_estimate=pl.CostEstimate(flops=2 * ROWS * D * FF, bytes_accessed=9000000, transcendentals=0),
        name="up_first",
    )(rows, *arrays)


def up_second(rows, before, arrays):
    return pl.pallas_call(
        up_second_kernel,
        in_specs=[pl.BlockSpec(memory_space=pl.ANY), pl.BlockSpec(memory_space=pltpu.VMEM)]
        + [pl.BlockSpec(memory_space=pl.ANY)] * 6,
        out_specs=pl.BlockSpec(memory_space=pltpu.VMEM),
        out_shape=jax.ShapeDtypeStruct((FF, 2 * ROWS), jnp.bfloat16),
        scratch_shapes=(pltpu.VMEM((2 * ROWS, FF), jnp.float32), *UP_SCRATCH),
        compiler_params=pltpu.CompilerParams(vmem_limit_bytes=VMEM_LIMIT),
        cost_estimate=pl.CostEstimate(flops=2 * ROWS * D * FF, bytes_accessed=11000000, transcendentals=ROWS * FF),
        name="up_second",
    )(rows, before, *arrays)


SENT_PARTS = ((7, 0, 640), (5, 0, 640), (4, 0, 640), (3, 320, 320), (2, 0, 320))
KEPT_PARTS = ((6, 0, 320), (6, 320, 320), (1, 0, 640), (3, 0, 320), (2, 320, 320), (0, 0, 640))


def down_kernel(parts, hidden, *refs):
    arrays, outs = refs[:18], refs[18 : 18 + len(parts)]
    hidden_v, weight_v, part_v, sems, out_sems = refs[18 + len(parts) :]
    load = pltpu.make_async_copy(hidden, hidden_v, sems.at[16])
    load.start()
    swaps = [RING[k] for k in (1, 2, 3, 4)] + [SIDE[k] for k in (1, 2, 3, 4)]
    for array, block, _, spot, _ in ring_blocks(1, START, swaps):
        target = weight_v.at[pl.ds(pl.multiple_of(spot * WBLK, 32), WBLK), :]
        copy = pltpu.make_async_copy(arrays[array].at[block], target, sems.at[spot // 2])
        first = spot % 4 * WBLK
        here = [(spot // 4 == k) & (first >= start) & (first < start + columns) for k, start, columns in parts]
        pl.when(functools.reduce(lambda p, q: p | q, here))(copy.start)
    copies = []
    load.wait()
    for n, (k, start, columns) in enumerate(parts):
        mine = pl.ds(k * COLS + start, columns)
        for first in range(start, start + columns, 2 * WBLK):
            two = pl.ds(k * COLS + first, 2 * WBLK)
            pltpu.make_async_copy(weight_v.at[two, :], weight_v.at[two, :], sems.at[2 * k + first // (2 * WBLK)]).wait()
        part = jnp.dot(weight_v[mine, :], hidden_v[...], preferred_element_type=jnp.float32)
        part_v[mine, :] = part.astype(jnp.bfloat16)
        copies.append(pltpu.make_async_copy(part_v.at[mine, :], outs[n], out_sems.at[n]))
        copies[-1].start()
    for copy in copies:
        copy.wait()


def down_product(hidden, arrays, parts):
    return pl.pallas_call(
        functools.partial(down_kernel, parts),
        in_specs=[pl.BlockSpec(memory_space=pl.ANY)] * (1 + len(arrays)),
        out_specs=[pl.BlockSpec(memory_space=pl.ANY)] * len(parts),
        out_shape=[jax.ShapeDtypeStruct((columns, 2 * ROWS), jnp.bfloat16) for _, _, columns in parts],
        scratch_shapes=[
            pltpu.VMEM((FF, 2 * ROWS), jnp.bfloat16),
            pltpu.VMEM((D, FF), jnp.bfloat16),
            pltpu.VMEM((D, 2 * ROWS), jnp.bfloat16),
            pltpu.SemaphoreType.DMA((17,)),
            pltpu.SemaphoreType.DMA((len(parts),)),
        ],
        compiler_params=pltpu.CompilerParams(vmem_limit_bytes=VMEM_LIMIT),
        cost_estimate=pl.CostEstimate(flops=2 * ROWS * D * FF, bytes_accessed=8000000, transcendentals=0),
        name="down_product",
    )(hidden, *arrays)


def added(*terms):
    return sum(t.astype(jnp.float32) for t in terms).astype(jnp.bfloat16)


def out_kernel(kept, partner, down, down_early, up_early, up, mod, tmod, block_out, block_tangent):
    outgate = mod[...].astype(jnp.float32)[2:3]
    toutgate = tmod[...].astype(jnp.float32)[2:3]
    half = COLS // 2
    for k in range(0, COLS, 64):
        cols = pl.ds(k, 64)
        late = pl.ds(k % half, 64)
        sides = (down, up_early) if k < half else (down_early, up)
        terms = [kept[cols, :], partner[cols, :], sides[0][late, :], sides[1][late, :]]
        tile = sum(t.astype(jnp.float32) for t in terms)
        if k % 128 == 0:
            before = tile
            continue
        tile = jnp.concatenate([before, tile], 0).T
        cols = pl.ds(k - 64, 128)
        mixed = tile[:ROWS]
        gate = outgate[:, k - 64 : k + 64]
        tgate = toutgate[:, k - 64 : k + 64]
        block_out[:, cols] = (gate * mixed).astype(jnp.bfloat16)
        block_tangent[:, cols] = (tgate * mixed + gate * tile[ROWS:]).astype(jnp.bfloat16)


def gated(terms, modulation, mod_tangent):
    return pl.pallas_call(
        out_kernel,
        in_specs=[pl.BlockSpec(memory_space=pltpu.VMEM)] * 8,
        out_specs=[pl.BlockSpec(memory_space=pltpu.VMEM)] * 2,
        out_shape=[jax.ShapeDtypeStruct((ROWS, COLS), jnp.bfloat16)] * 2,
        compiler_params=pltpu.CompilerParams(vmem_limit_bytes=VMEM_LIMIT),
        cost_estimate=pl.CostEstimate(flops=10 * ROWS * COLS, bytes_accessed=3500000, transcendentals=0),
        name="gated",
    )(*terms, modulation, mod_tangent)


def shards(tokens, tangent, modulation, mod_tangent, up_weight, down_weight):
    own = packed(tokens, tangent, modulation, mod_tangent)
    mine = jnp.stack([down_weight.T, up_weight])

    other = core_swap(mine)
    far = y_far(mine[1:])
    from_low = x_up(own)
    from_high = x_down(own)
    near = y_near(after(own, far))
    m1 = z_ring(jnp.concatenate([other[1:], other[:1], mine], 0))
    far_other = core_swap(far)
    m1, far, far_other, from_low, from_high, near = fence(m1, far, far_other, from_low, from_high, near)

    near_low = x_up(near)
    near_high = x_down(near)
    m2 = z_ring(jnp.concatenate([m1, far, far_other], 0))
    s1 = core_swap(m1)
    q1 = y_far(jnp.concatenate([mine[:1], m1[1:3]], 0))
    m2, s1, q1, near_low, near_high = fence(m2, s1, q1, near_low, near_high)

    across_low = x_up(jnp.concatenate([from_low[:ROWS], near_low[:ROWS]], 0))
    across_high = x_down(jnp.concatenate([from_high[ROWS:], near_high[ROWS:]], 0))
    m3 = z_ring(m2)
    q2 = y_far(m2[1:3])
    s2 = core_swap(m2)
    m3, s2, q2, across_low, across_high = fence(m3, s2, q2, across_low, across_high)

    m4 = z_ring(m3[2:])
    q3 = y_far(m3[1:3])
    s3 = core_swap(m3)
    t1 = core_swap(q1)
    rows = shape_rows([own, near, from_low, from_high, near_low, near_high], across_low, across_high)
    rows = rows.reshape(2 * ROWS, D)
    m4, q3, s3, t1, rows = fence(m4, q3, s3, t1, rows)

    m5 = z_ring(m4[2:3])
    q4 = y_far(m4[:1])
    s4 = core_swap(m4)
    t2 = core_swap(q2)
    start = [mine, other]
    total = up_first(rows, [*start, far, far_other, m1, s1, m2, s2, m3, s3])
    m5, s4, t2, q4, total = fence(m5, s4, t2, q4, total)

    s5 = core_swap(m5)
    hidden = up_second(rows, total, [m3, s3, m4, s4, m5, s5])
    t3 = core_swap(q3)
    t4 = core_swap(q4)
    t3, t4, hidden = fence(t3, t4, hidden)

    arrays = [*start, m1, s1, m2, s2, m3, s3, m4, s4, q1, t1, q2, t2, q3, t3, q4, t4]
    first = down_product(hidden, arrays, SENT_PARTS)
    from_near = y_near(first[0])
    near_from_low = x_up(first[1])
    near_from_high = x_down(first[2])
    from_down_early = x_up(first[3])
    from_up_early = x_down(first[4])
    rest = down_product(after(hidden, first[0]), arrays, KEPT_PARTS)
    far_up, far_down, partner, to_high, to_low, kept = rest
    half = COLS // 2
    from_far_low = x_up(added(far_up, from_near[:half]))
    from_far_high = x_down(added(far_down, from_near[half:]))
    from_partner = y_near(added(partner, near_from_low, near_from_high))
    from_down = x_up(added(to_high, from_far_low))
    from_up = x_down(added(to_low, from_far_high))
    terms = [kept, from_partner, from_down, from_down_early, from_up_early, from_up]
    block_out, block_tangent = gated(terms, modulation, mod_tangent)
    return (block_out, block_tangent)


def solution(mesh):
    return jax.shard_map(
        shards,
        mesh=mesh,
        in_specs=(
            P("ctx", "tp"),
            P("ctx", "tp"),
            P(None, "tp"),
            P(None, "tp"),
            P("ctx", "tp"),
            P("tp", "ctx"),
        ),
        out_specs=(P("ctx", "tp"), P("ctx", "tp")),
        check_vma=False,
    )
```

```python
import functools
import math

import jax
import jax.numpy as jnp
from jax import lax
from jax.experimental import pallas as pl
from jax.experimental.pallas import tpu as pltpu
from jax.sharding import PartitionSpec as P

D = 5120
ROWS = 256
COLS = 640
FF = 864
WBLK = 160
VMEM_LIMIT = 56 * 1024 * 1024


def ctx_perm(move):
    pairs = []
    for i in range(32):
        h, z, c = move(i // 16, (i // 2) % 8, i % 2)
        pairs.append((i, ((h % 2) * 8 + z % 8) * 2 + c % 2))
    return pairs


def tp_perm(move):
    pairs = []
    for i in range(8):
        x, y = move(i // 2, i % 2)
        pairs.append((i, (x % 4) * 2 + y % 2))
    return pairs


def x_up(v):
    return lax.ppermute(v, "tp", tp_perm(lambda x, y: (x + 1, y)))


def x_down(v):
    return lax.ppermute(v, "tp", tp_perm(lambda x, y: (x - 1, y)))


def y_near(v):
    return lax.ppermute(v, "tp", tp_perm(lambda x, y: (x, y + 1)))


def y_far(v):
    return lax.ppermute(v, "ctx", ctx_perm(lambda h, z, c: (h + 1, z, c)))


def core_swap(v):
    return lax.ppermute(v, "ctx", ctx_perm(lambda h, z, c: (h, z, c + 1)))


def z_ring(v):
    return lax.ppermute(v, "ctx", ctx_perm(lambda h, z, c: (h, z + 1 - 2 * c, c)))


def place():
    t = lax.axis_index("tp")
    i = lax.axis_index("ctx")
    return t // 2, t % 2, i // 16, (i // 2) % 8, i % 2


def near_order(x, y, h, z):
    owner = h * 4 + z // 2
    dx = (owner // 2 - x + 4) % 4
    dy = (owner % 2 - y + 2) % 2
    side = jnp.where(dx == 3, 2, 3) + 2 * dy
    return jnp.where(dx == 0, dy, jnp.where(dx == 2, 6 + dy, side))


def after(value, *others):
    return lax.optimization_barrier((value, *others))[0]


def fence(*values):
    return lax.optimization_barrier(values)


START = tuple(((1, 0, 0, own), (0, 0, 0, own)) for own in (1, 0))
FAR_START = tuple(((0, 1, 0, own),) for own in (1, 0))


def ring_step(step):
    blocks = ((0, 0, step, 0), (1, 0, step, 0), (1, 0, step, 1), (0, 0, step, 1))
    if step > 1:
        blocks += ((0, 1, step - 1, 1), (0, 1, step - 1, 0))
    return blocks


RING = {k: ring_step(k) for k in (1, 2, 3)}
RING[4] = ((1, 0, 4, 1), (0, 0, 4, 1), (0, 1, 3, 1), (0, 1, 3, 0))
RING[5] = ((0, 1, 4, 1),)
SIDE = {k: ((1, 1, k, 0), (1, 1, k, 1)) for k in (1, 2, 3)}
SIDE[1] = ((1, 1, 0, 1), *SIDE[1])
SIDE[4] = ((1, 1, 4, 1),)


def ring_blocks(kind, sources, swaps):
    x, y, h, z, c = place()
    out = []
    arrays = [(blocks, False) for blocks in sources]
    for blocks in swaps:
        arrays += [(blocks, False), (blocks, True)]
    for array, (blocks, swapped) in enumerate(arrays):
        for block, (of, stream, step, own) in enumerate(blocks):
            if of != kind:
                continue
            sign = 1 - 2 * c
            there = (z + (step * sign if swapped else -step * sign) + 8) % 8
            core = c if bool(own) != swapped else 1 - c
            spot = near_order(x, y, 1 - h if stream else h, there) * 4 + (there % 2) * 2 + core
            out.append((array, block, stream, spot, there // 2))
    return out


def pack_kernel(tokens, tangent, modulation, mod_tangent, out):
    out[:ROWS, :] = tokens[...]
    out[ROWS : 2 * ROWS, :] = tangent[...]
    mods = [modulation[...].astype(jnp.float32), mod_tangent[...].astype(jnp.float32)]
    tail = jnp.concatenate([*mods, jnp.zeros((10, COLS), jnp.float32)], 0)
    out[2 * ROWS :, :] = tail.astype(jnp.bfloat16)


def packed(*arrays):
    return pl.pallas_call(
        pack_kernel,
        in_specs=[pl.BlockSpec(memory_space=pltpu.VMEM)] * 4,
        out_specs=pl.BlockSpec(memory_space=pltpu.VMEM),
        out_shape=jax.ShapeDtypeStruct((2 * ROWS + 16, COLS), jnp.bfloat16),
        cost_estimate=pl.CostEstimate(flops=10**11, bytes_accessed=1400000, transcendentals=0),
        name="packed",
    )(*arrays)


def shape_kernel(*refs):
    whole, across_low, across_high, out = refs[:6], refs[6], refs[7], refs[8]
    toks = [(r, 0) for r in whole] + [(across_low, 0), (across_low, ROWS)]
    tans = [(r, ROWS) for r in whole] + [(across_high, 0), (across_high, ROWS + 16)]
    spread = refs[9]
    lanes = [(k, pl.ds(n, 128), k * COLS + n) for k in range(8) for n in range(0, COLS, 128)]
    tile = out.shape[1]

    @pl.when(pl.program_id(0) == 0)
    def _():
        for k, cols, first in lanes:
            ref, base = tans[k]
            mod = ref[pl.ds(base + ROWS, 16), cols].astype(jnp.float32)
            for n, row in enumerate((mod[0:1], 1.0 + mod[1:2], mod[3:4], mod[4:5])):
                spread[n, :, pl.ds(first, 128)] = jnp.broadcast_to(row, (16, 128))

    start = pl.program_id(0) * tile

    def load(source, k, cols, first):
        ref, base = source[k]
        return ref[pl.ds(pl.multiple_of(base + first, 16), 16), cols].astype(jnp.float32)

    def sixteen(i, carry):
        first = start + i * 16
        sums = [jnp.zeros((16, 128), jnp.float32) for _ in range(4)]
        for k, cols, _ in lanes:
            t = load(toks, k, cols, first)
            u = load(tans, k, cols, first)
            sums = [sums[0] + t, sums[1] + t * t, sums[2] + u, sums[3] + t * u]
        row_sum, square_sum, tan_sum, cross_sum = [jnp.sum(p, axis=1, keepdims=True) for p in sums]
        row_mean = row_sum / D
        inverse_std = lax.rsqrt(square_sum / D - row_mean * row_mean + 1e-06)
        tan_mean = tan_sum / D
        crossed = (cross_sum / D - row_mean * tan_mean) * inverse_std
        back = crossed * inverse_std
        rows = pl.ds(pl.multiple_of(i * 16, 16), 16)
        for k, cols, place_of in lanes:
            target = pl.ds(place_of, 128)
            shift, gain, tshift, tscale = (spread[n, :, target] for n in range(4))
            normed = (load(toks, k, cols, first) - row_mean) * inverse_std
            tnormed = (load(tans, k, cols, first) - tan_mean) * inverse_std - normed * back
            out[0, rows, target] = (normed * gain + shift).astype(jnp.bfloat16)
            out[1, rows, target] = (tnormed * gain + normed * tscale + tshift).astype(jnp.bfloat16)
        return carry

    lax.fori_loop(0, tile // 16, sixteen, 0)


def shape_rows(whole, across_low, across_high):
    tile = 64
    sources = [*whole, across_low, across_high]
    return pl.pallas_call(
        shape_kernel,
        grid=(ROWS // tile,),
        in_specs=[pl.BlockSpec(a.shape, lambda i: (0, 0)) for a in sources],
        out_specs=pl.BlockSpec((2, tile, D), lambda i: (0, i, 0)),
        out_shape=jax.ShapeDtypeStruct((2, ROWS, D), jnp.bfloat16),
        scratch_shapes=[pltpu.VMEM((4, 16, D), jnp.float32)],
        compiler_params=pltpu.CompilerParams(vmem_limit_bytes=VMEM_LIMIT),
        cost_estimate=pl.CostEstimate(flops=30 * ROWS * D, bytes_accessed=8 * ROWS * D, transcendentals=0),
        name="shape_rows",
    )(*sources)


def feature_products(rows, arrays, blocks, wanted, groups, rows_v, weight_v, row_sems, weight_sems):
    x, y, h, _, _ = place()
    order = [near_order(x, y, 1 - h if stream else h, 2 * pair) for stream, pair in wanted]

    def row_copy(n):
        cols = pl.ds(pl.multiple_of(order[n] * COLS, 128), COLS)
        return pltpu.make_async_copy(rows.at[:, cols], rows_v.at[:, pl.ds(n * COLS, COLS)], row_sems.at[n])

    for n in range(len(order)):
        row_copy(n).start()
    for array, block, stream, spot, pair in blocks:
        here = [(n, pair == other) for n, (of, other) in enumerate(wanted) if of == stream]
        slot = sum(jnp.where(same, n, 0) for n, same in here)
        target = weight_v.at[pl.ds(pl.multiple_of(slot * COLS + spot % 4 * WBLK, 32), WBLK), :]
        copy = pltpu.make_async_copy(arrays[array].at[block], target, weight_sems.at[slot])
        pl.when(functools.reduce(lambda p, q: p | q, [same for _, same in here]))(copy.start)
    first = 0
    for group in groups:
        for n in range(first, first + group):
            row_copy(n).wait()
            block = weight_v.at[pl.ds(n * COLS, COLS), :]
            pltpu.make_async_copy(block, block, weight_sems.at[n]).wait()
        span = pl.ds(first * COLS, group * COLS)
        yield jnp.dot(rows_v[:, span], weight_v[span, :], preferred_element_type=jnp.float32)
        first += group


def pair_order():
    z = place()[3]
    side = 2 * (z % 2) - 1
    return [z // 2, (z // 2 + side + 4) % 4, (z // 2 - side + 4) % 4, (z // 2 + 2) % 4]


def up_first_kernel(rows, *refs):
    arrays, total, scratch = refs[:10], refs[10], refs[11:]
    p = pair_order()
    wanted = [(0, p[0]), (0, p[1]), (1, p[0]), (0, p[2]), (1, p[1])]
    blocks = ring_blocks(0, START + FAR_START, [RING[k] for k in (1, 2, 3)])
    first, second = feature_products(rows, arrays, blocks, wanted, (3, 2), *scratch)
    total[...] = first
    total[...] += second


def up_second_kernel(rows, before, *refs):
    arrays, out, total, before_sem, scratch = refs[:6], refs[6], refs[7], refs[8], refs[9:]
    load = pltpu.make_async_copy(before, total, before_sem)
    load.start()
    p = pair_order()
    wanted = [(1, p[2]), (0, p[3]), (1, p[3])]
    blocks = ring_blocks(0, (), [RING[k] for k in (3, 4, 5)])
    (part,) = feature_products(rows, arrays, blocks, wanted, (3,), *scratch)
    load.wait()
    total[...] += part
    coeff = math.sqrt(2.0 / math.pi)
    tile = 16

    def activate(k, carry):
        now = pl.ds(pl.multiple_of(k * tile, tile), tile)
        later = pl.ds(pl.multiple_of(ROWS + k * tile, tile), tile)
        up = total[now, :]
        square = up * up
        th = jnp.tanh(coeff * (up + 0.044715 * up * square))
        half = 0.5 * (1.0 + th)
        slopes = half + 0.5 * up * (1.0 - th * th) * coeff * (1.0 + 3.0 * 0.044715 * square)
        total[later, :] = slopes * total[later, :]
        total[now, :] = up * half
        return carry

    lax.fori_loop(0, ROWS // tile, activate, 0)
    for k in range(0, FF, 128):
        width = min(128, FF - k)
        out[pl.ds(k, width), :] = total[:, pl.ds(k, width)].T.astype(jnp.bfloat16)


def up_scratch(count):
    return (
        pltpu.VMEM((2 * ROWS, count * COLS), jnp.bfloat16),
        pltpu.VMEM((count * COLS, FF), jnp.bfloat16),
        pltpu.SemaphoreType.DMA((count,)),
        pltpu.SemaphoreType.DMA((count,)),
    )


def up_first(rows, arrays):
    return pl.pallas_call(
        up_first_kernel,
        in_specs=[pl.BlockSpec(memory_space=pl.ANY)] * 11,
        out_specs=pl.BlockSpec(memory_space=pltpu.VMEM),
        out_shape=jax.ShapeDtypeStruct((2 * ROWS, FF), jnp.float32),
        scratch_shapes=up_scratch(5),
        compiler_params=pltpu.CompilerParams(vmem_limit_bytes=VMEM_LIMIT),
        cost_estimate=pl.CostEstimate(flops=2 * ROWS * D * FF, bytes_accessed=9000000, transcendentals=0),
        name="up_first",
    )(rows, *arrays)


def up_second(rows, before, arrays):
    return pl.pallas_call(
        up_second_kernel,
        in_specs=[pl.BlockSpec(memory_space=pl.ANY)] * 8,
        out_specs=pl.BlockSpec(memory_space=pltpu.VMEM),
        out_shape=jax.ShapeDtypeStruct((FF, 2 * ROWS), jnp.bfloat16),
        scratch_shapes=(pltpu.VMEM((2 * ROWS, FF), jnp.float32), pltpu.SemaphoreType.DMA, *up_scratch(3)),
        compiler_params=pltpu.CompilerParams(vmem_limit_bytes=VMEM_LIMIT),
        cost_estimate=pl.CostEstimate(flops=2 * ROWS * D * FF, bytes_accessed=11000000, transcendentals=ROWS * FF),
        name="up_second",
    )(rows, before, *arrays)


SENT_PARTS = ((7, 0, 320), (7, 320, 320), (5, 0, 640), (4, 0, 640))
KEPT_PARTS = (
    (6, 0, 320),
    (6, 320, 320),
    (1, 0, 640),
    (3, 0, 320),
    (3, 320, 320),
    (2, 0, 320),
    (2, 320, 320),
    (0, 0, 640),
)


def down_kernel(parts, hidden, *refs):
    arrays, outs = refs[:18], refs[18 : 18 + len(parts)]
    hidden_v, weight_v, part_v, sems, out_sems = refs[18 + len(parts) :]
    load = pltpu.make_async_copy(hidden, hidden_v, sems.at[16])
    load.start()
    swaps = [RING[k] for k in (1, 2, 3, 4)] + [SIDE[k] for k in (1, 2, 3, 4)]
    for array, block, _, spot, _ in ring_blocks(1, START, swaps):
        target = weight_v.at[pl.ds(pl.multiple_of(spot * WBLK, 32), WBLK), :]
        copy = pltpu.make_async_copy(arrays[array].at[block], target, sems.at[spot // 2])
        first = spot % 4 * WBLK
        here = [(spot // 4 == k) & (first >= start) & (first < start + columns) for k, start, columns in parts]
        pl.when(functools.reduce(lambda p, q: p | q, here))(copy.start)
    copies = []
    load.wait()
    for n, (k, start, columns) in enumerate(parts):
        mine = pl.ds(k * COLS + start, columns)
        for first in range(start, start + columns, 2 * WBLK):
            two = pl.ds(k * COLS + first, 2 * WBLK)
            pltpu.make_async_copy(weight_v.at[two, :], weight_v.at[two, :], sems.at[2 * k + first // (2 * WBLK)]).wait()
        part = jnp.dot(weight_v[mine, :], hidden_v[...], preferred_element_type=jnp.float32)
        part_v[mine, :] = part.astype(jnp.bfloat16)
        copies.append(pltpu.make_async_copy(part_v.at[mine, :], outs[n], out_sems.at[n]))
        copies[-1].start()
    for copy in copies:
        copy.wait()


def down_product(hidden, arrays, parts):
    return pl.pallas_call(
        functools.partial(down_kernel, parts),
        in_specs=[pl.BlockSpec(memory_space=pl.ANY)] * (1 + len(arrays)),
        out_specs=[pl.BlockSpec(memory_space=pl.ANY)] * len(parts),
        out_shape=[jax.ShapeDtypeStruct((columns, 2 * ROWS), jnp.bfloat16) for _, _, columns in parts],
        scratch_shapes=[
            pltpu.VMEM((FF, 2 * ROWS), jnp.bfloat16),
            pltpu.VMEM((D, FF), jnp.bfloat16),
            pltpu.VMEM((D, 2 * ROWS), jnp.bfloat16),
            pltpu.SemaphoreType.DMA((17,)),
            pltpu.SemaphoreType.DMA((len(parts),)),
        ],
        compiler_params=pltpu.CompilerParams(vmem_limit_bytes=VMEM_LIMIT),
        cost_estimate=pl.CostEstimate(flops=2 * ROWS * D * FF, bytes_accessed=8000000, transcendentals=0),
        name="down_product",
    )(hidden, *arrays)


def added(*terms):
    return sum(t.astype(jnp.float32) for t in terms).astype(jnp.bfloat16)


def out_kernel(kept, partner, down, down_early, up_early, up, mod, tmod, block_out, block_tangent):
    outgate = mod[...].astype(jnp.float32)[2:3]
    toutgate = tmod[...].astype(jnp.float32)[2:3]
    half = COLS // 2
    for k in range(0, COLS, 64):
        cols = pl.ds(k, 64)
        late = pl.ds(k % half, 64)
        sides = (down, up_early) if k < half else (down_early, up)
        terms = [kept[cols, :], partner[cols, :], sides[0][late, :], sides[1][late, :]]
        tile = sum(t.astype(jnp.float32) for t in terms)
        if k % 128 == 0:
            before = tile
            continue
        tile = jnp.concatenate([before, tile], 0).T
        cols = pl.ds(k - 64, 128)
        mixed = tile[:ROWS]
        gate = outgate[:, k - 64 : k + 64]
        tgate = toutgate[:, k - 64 : k + 64]
        block_out[:, cols] = (gate * mixed).astype(jnp.bfloat16)
        block_tangent[:, cols] = (tgate * mixed + gate * tile[ROWS:]).astype(jnp.bfloat16)


def gated(terms, modulation, mod_tangent):
    return pl.pallas_call(
        out_kernel,
        in_specs=[pl.BlockSpec(memory_space=pltpu.VMEM)] * 8,
        out_specs=[pl.BlockSpec(memory_space=pltpu.VMEM)] * 2,
        out_shape=[jax.ShapeDtypeStruct((ROWS, COLS), jnp.bfloat16)] * 2,
        compiler_params=pltpu.CompilerParams(vmem_limit_bytes=VMEM_LIMIT),
        cost_estimate=pl.CostEstimate(flops=10 * ROWS * COLS, bytes_accessed=3500000, transcendentals=0),
        name="gated",
    )(*terms, modulation, mod_tangent)


def shards(tokens, tangent, modulation, mod_tangent, up_weight, down_weight):
    own = packed(tokens, tangent, modulation, mod_tangent)
    mine = jnp.stack([down_weight.T, up_weight])

    other = core_swap(mine)
    far = y_far(up_weight)[None]
    from_low = x_up(own)
    from_high = x_down(own)
    near = y_near(after(own, far))
    m1 = z_ring(jnp.concatenate([other[1:], other[:1], mine], 0))
    far_other = core_swap(far)
    m1, far, far_other, from_low, from_high, near = fence(m1, far, far_other, from_low, from_high, near)

    near_low = x_up(near)
    near_high = x_down(near)
    m2 = z_ring(jnp.concatenate([m1, far, far_other], 0))
    s1 = core_swap(m1)
    q1 = y_far(after(jnp.concatenate([mine[:1], m1[1:3]], 0), s1))
    m2, s1, q1, near_low, near_high = fence(m2, s1, q1, near_low, near_high)

    across_low = x_up(jnp.concatenate([from_low[:ROWS], near_low[:ROWS]], 0))
    across_high = x_down(jnp.concatenate([from_high[ROWS:], near_high[ROWS:]], 0))
    m3 = z_ring(m2)
    q2 = y_far(m2[1:3])
    s2 = core_swap(m2)
    m3, s2, q2, across_low, across_high = fence(m3, s2, q2, across_low, across_high)

    m4 = z_ring(m3[2:])
    q3 = y_far(m3[1:3])
    s3 = core_swap(m3)
    t1 = core_swap(q1)
    rows = shape_rows([own, near, from_low, from_high, near_low, near_high], across_low, across_high)
    rows = rows.reshape(2 * ROWS, D)
    m4, q3, s3, t1, rows = fence(m4, q3, s3, t1, rows)

    m5 = z_ring(m4[2:3])
    q4 = y_far(m4[:1])
    s4 = core_swap(m4)
    t2 = core_swap(q2)
    start = [mine, other]
    total = up_first(rows, [*start, far, far_other, m1, s1, m2, s2, m3, s3])
    m5, s4, t2, q4, total = fence(m5, s4, t2, q4, total)

    s5 = core_swap(m5)
    t3 = core_swap(q3)
    t4 = core_swap(q4)
    s5, t3, t4, total = fence(s5, t3, t4, total)
    hidden = up_second(rows, total, [m3, s3, m4, s4, m5, s5])

    arrays = [*start, m1, s1, m2, s2, m3, s3, m4, s4, q1, t1, q2, t2, q3, t3, q4, t4]
    first = down_product(hidden, arrays, SENT_PARTS)
    from_near = [y_near(first[0]), y_near(first[1])]
    near_from_low = x_up(first[2])
    near_from_high = x_down(first[3])
    rest = down_product(after(hidden, first[0]), arrays, KEPT_PARTS)
    from_near[0], rest = lax.optimization_barrier((from_near[0], rest))
    far_up, far_down, partner, to_high, stay_high, stay_low, to_low, kept = rest
    from_far_low = x_up(added(far_up, from_near[0]))
    from_far_high = x_down(added(far_down, from_near[1]))
    from_partner = y_near(added(partner, near_from_low, near_from_high))
    from_down_early = x_up(stay_high)
    from_up_early = x_down(stay_low)
    from_down = x_up(added(to_high, from_far_low))
    from_up = x_down(added(to_low, from_far_high))
    terms = [kept, from_partner, from_down, from_down_early, from_up_early, from_up]
    block_out, block_tangent = gated(terms, modulation, mod_tangent)
    return (block_out, block_tangent)


def solution(mesh):
    return jax.shard_map(
        shards,
        mesh=mesh,
        in_specs=(
            P("ctx", "tp"),
            P("ctx", "tp"),
            P(None, "tp"),
            P(None, "tp"),
            P("ctx", "tp"),
            P("tp", "ctx"),
        ),
        out_specs=(P("ctx", "tp"), P("ctx", "tp")),
        check_vma=False,
    )
```

```python
import functools
import math

import jax
import jax.numpy as jnp
from jax import lax
from jax.experimental import pallas as pl
from jax.experimental.pallas import tpu as pltpu
from jax.sharding import PartitionSpec as P

D = 5120
ROWS = 256
COLS = 640
FF = 864
WBLK = 160
VMEM_LIMIT = 56 * 1024 * 1024


def ctx_perm(move):
    pairs = []
    for i in range(32):
        h, z, c = move(i // 16, (i // 2) % 8, i % 2)
        pairs.append((i, ((h % 2) * 8 + z % 8) * 2 + c % 2))
    return pairs


def tp_perm(move):
    pairs = []
    for i in range(8):
        x, y = move(i // 2, i % 2)
        pairs.append((i, (x % 4) * 2 + y % 2))
    return pairs


def x_up(v):
    return lax.ppermute(v, "tp", tp_perm(lambda x, y: (x + 1, y)))


def x_down(v):
    return lax.ppermute(v, "tp", tp_perm(lambda x, y: (x - 1, y)))


def y_near(v):
    return lax.ppermute(v, "tp", tp_perm(lambda x, y: (x, y + 1)))


def y_far(v):
    return lax.ppermute(v, "ctx", ctx_perm(lambda h, z, c: (h + 1, z, c)))


def core_swap(v):
    return lax.ppermute(v, "ctx", ctx_perm(lambda h, z, c: (h, z, c + 1)))


def z_ring(v):
    return lax.ppermute(v, "ctx", ctx_perm(lambda h, z, c: (h, z + 1 - 2 * c, c)))


def place():
    t = lax.axis_index("tp")
    i = lax.axis_index("ctx")
    return t // 2, t % 2, i // 16, (i // 2) % 8, i % 2


def near_order(x, y, h, z):
    owner = h * 4 + z // 2
    dx = (owner // 2 - x + 4) % 4
    dy = (owner % 2 - y + 2) % 2
    side = jnp.where(dx == 3, 2, 3) + 2 * dy
    return jnp.where(dx == 0, dy, jnp.where(dx == 2, 6 + dy, side))


def after(value, *others):
    return lax.optimization_barrier((value, *others))[0]


def fence(*values):
    return lax.optimization_barrier(values)


START = tuple(((1, 0, 0, own), (0, 0, 0, own)) for own in (1, 0))
FAR_START = tuple(((0, 1, 0, own),) for own in (1, 0))


def ring_step(step):
    blocks = ((0, 0, step, 0), (1, 0, step, 0), (1, 0, step, 1), (0, 0, step, 1))
    if step > 1:
        blocks += ((0, 1, step - 1, 1), (0, 1, step - 1, 0))
    return blocks


RING = {k: ring_step(k) for k in (1, 2, 3)}
RING[4] = ((1, 0, 4, 1), (0, 0, 4, 1), (0, 1, 3, 1), (0, 1, 3, 0))
RING[5] = ((0, 1, 4, 1),)
SIDE = {k: ((1, 1, k, 0), (1, 1, k, 1)) for k in (1, 2, 3)}
SIDE[1] = ((1, 1, 0, 1), *SIDE[1])
SIDE[4] = ((1, 1, 4, 1),)


def ring_blocks(kind, sources, swaps):
    x, y, h, z, c = place()
    out = []
    arrays = [(blocks, False) for blocks in sources]
    for blocks in swaps:
        arrays += [(blocks, False), (blocks, True)]
    for array, (blocks, swapped) in enumerate(arrays):
        for block, (of, stream, step, own) in enumerate(blocks):
            if of != kind:
                continue
            sign = 1 - 2 * c
            there = (z + (step * sign if swapped else -step * sign) + 8) % 8
            core = c if bool(own) != swapped else 1 - c
            spot = near_order(x, y, 1 - h if stream else h, there) * 4 + (there % 2) * 2 + core
            out.append((array, block, stream, spot, there // 2))
    return out


def pack_kernel(tokens, tangent, modulation, mod_tangent, out):
    out[:ROWS, :] = tokens[...]
    out[ROWS : 2 * ROWS, :] = tangent[...]
    mods = [modulation[...].astype(jnp.float32), mod_tangent[...].astype(jnp.float32)]
    tail = jnp.concatenate([*mods, jnp.zeros((10, COLS), jnp.float32)], 0)
    out[2 * ROWS :, :] = tail.astype(jnp.bfloat16)


def packed(*arrays):
    return pl.pallas_call(
        pack_kernel,
        in_specs=[pl.BlockSpec(memory_space=pltpu.VMEM)] * 4,
        out_specs=pl.BlockSpec(memory_space=pltpu.VMEM),
        out_shape=jax.ShapeDtypeStruct((2 * ROWS + 16, COLS), jnp.bfloat16),
        cost_estimate=pl.CostEstimate(flops=10**11, bytes_accessed=1400000, transcendentals=0),
        name="packed",
    )(*arrays)


def shape_kernel(*refs):
    whole, across_low, across_high, out = refs[:6], refs[6], refs[7], refs[8]
    toks = [(r, 0) for r in whole] + [(across_low, 0), (across_low, ROWS)]
    tans = [(r, ROWS) for r in whole] + [(across_high, 0), (across_high, ROWS + 16)]
    spread = refs[9]
    lanes = [(k, pl.ds(n, 128), k * COLS + n) for k in range(8) for n in range(0, COLS, 128)]
    tile = out.shape[1]

    @pl.when(pl.program_id(0) == 0)
    def _():
        for k, cols, first in lanes:
            ref, base = tans[k]
            mod = ref[pl.ds(base + ROWS, 16), cols].astype(jnp.float32)
            for n, row in enumerate((mod[0:1], 1.0 + mod[1:2], mod[3:4], mod[4:5])):
                spread[n, :, pl.ds(first, 128)] = jnp.broadcast_to(row, (16, 128))

    start = pl.program_id(0) * tile

    def load(source, k, cols, first):
        ref, base = source[k]
        return ref[pl.ds(pl.multiple_of(base + first, 16), 16), cols].astype(jnp.float32)

    def sixteen(i, carry):
        first = start + i * 16
        sums = [jnp.zeros((16, 128), jnp.float32) for _ in range(4)]
        for k, cols, _ in lanes:
            t = load(toks, k, cols, first)
            u = load(tans, k, cols, first)
            sums = [sums[0] + t, sums[1] + t * t, sums[2] + u, sums[3] + t * u]
        row_sum, square_sum, tan_sum, cross_sum = [jnp.sum(p, axis=1, keepdims=True) for p in sums]
        row_mean = row_sum / D
        inverse_std = lax.rsqrt(square_sum / D - row_mean * row_mean + 1e-06)
        tan_mean = tan_sum / D
        crossed = (cross_sum / D - row_mean * tan_mean) * inverse_std
        back = crossed * inverse_std
        rows = pl.ds(pl.multiple_of(i * 16, 16), 16)
        for k, cols, place_of in lanes:
            target = pl.ds(place_of, 128)
            shift, gain, tshift, tscale = (spread[n, :, target] for n in range(4))
            normed = (load(toks, k, cols, first) - row_mean) * inverse_std
            tnormed = (load(tans, k, cols, first) - tan_mean) * inverse_std - normed * back
            out[0, rows, target] = (normed * gain + shift).astype(jnp.bfloat16)
            out[1, rows, target] = (tnormed * gain + normed * tscale + tshift).astype(jnp.bfloat16)
        return carry

    lax.fori_loop(0, tile // 16, sixteen, 0)


def shape_rows(whole, across_low, across_high):
    tile = 64
    sources = [*whole, across_low, across_high]
    return pl.pallas_call(
        shape_kernel,
        grid=(ROWS // tile,),
        in_specs=[pl.BlockSpec(a.shape, lambda i: (0, 0)) for a in sources],
        out_specs=pl.BlockSpec((2, tile, D), lambda i: (0, i, 0)),
        out_shape=jax.ShapeDtypeStruct((2, ROWS, D), jnp.bfloat16),
        scratch_shapes=[pltpu.VMEM((4, 16, D), jnp.float32)],
        compiler_params=pltpu.CompilerParams(vmem_limit_bytes=VMEM_LIMIT),
        cost_estimate=pl.CostEstimate(flops=30 * ROWS * D, bytes_accessed=8 * ROWS * D, transcendentals=0),
        name="shape_rows",
    )(*sources)


def feature_products(rows, arrays, blocks, wanted, groups, rows_v, weight_v, row_sems, weight_sems):
    x, y, h, _, _ = place()
    order = [near_order(x, y, 1 - h if stream else h, 2 * pair) for stream, pair in wanted]

    def row_copy(n):
        cols = pl.ds(pl.multiple_of(order[n] * COLS, 128), COLS)
        return pltpu.make_async_copy(rows.at[:, cols], rows_v.at[:, pl.ds(n * COLS, COLS)], row_sems.at[n])

    for n in range(len(order)):
        row_copy(n).start()
    for array, block, stream, spot, pair in blocks:
        here = [(n, pair == other) for n, (of, other) in enumerate(wanted) if of == stream]
        slot = sum(jnp.where(same, n, 0) for n, same in here)
        target = weight_v.at[pl.ds(pl.multiple_of(slot * COLS + spot % 4 * WBLK, 32), WBLK), :]
        copy = pltpu.make_async_copy(arrays[array].at[block], target, weight_sems.at[slot])
        pl.when(functools.reduce(lambda p, q: p | q, [same for _, same in here]))(copy.start)
    yield None
    first = 0
    for group in groups:
        for n in range(first, first + group):
            row_copy(n).wait()
            block = weight_v.at[pl.ds(n * COLS, COLS), :]
            pltpu.make_async_copy(block, block, weight_sems.at[n]).wait()
        span = pl.ds(first * COLS, group * COLS)
        yield jnp.dot(rows_v[:, span], weight_v[span, :], preferred_element_type=jnp.float32)
        first += group


def pair_order():
    z = place()[3]
    side = 2 * (z % 2) - 1
    return [z // 2, (z // 2 + side + 4) % 4, (z // 2 - side + 4) % 4, (z // 2 + 2) % 4]


def up_first_kernel(rows, *refs):
    arrays, total, scratch = refs[:10], refs[10], refs[11:]
    p = pair_order()
    wanted = [(0, p[0]), (0, p[1]), (1, p[0]), (0, p[2]), (1, p[1])]
    blocks = ring_blocks(0, START + FAR_START, [RING[k] for k in (1, 2, 3)])
    _, first, second = feature_products(rows, arrays, blocks, wanted, (3, 2), *scratch)
    total[...] = first
    total[...] += second


def up_second_kernel(rows, before, *refs):
    arrays, last, hidden, parts = refs[:18], refs[18:20], refs[20], refs[21:25]
    hidden_v, hidden_sem, weight_v, part_v, down_sems, out_sems, total, before_sem = refs[25:33]
    p = pair_order()
    wanted = [(1, p[2]), (0, p[3]), (1, p[3])]
    blocks = ring_blocks(0, (), [RING[k] for k in (3, 4, 5)])
    products = feature_products(rows, [*arrays[6:10], *last], blocks, wanted, (3,), *refs[33:])
    next(products)
    load = pltpu.make_async_copy(before, total, before_sem)
    load.start()
    start_down(SENT_PARTS, arrays, weight_v, down_sems)
    (part,) = products
    load.wait()
    total[...] += part
    coeff = math.sqrt(2.0 / math.pi)
    tile = 16

    def activate(k, carry):
        now = pl.ds(pl.multiple_of(k * tile, tile), tile)
        later = pl.ds(pl.multiple_of(ROWS + k * tile, tile), tile)
        up = total[now, :]
        square = up * up
        th = jnp.tanh(coeff * (up + 0.044715 * up * square))
        half = 0.5 * (1.0 + th)
        slopes = half + 0.5 * up * (1.0 - th * th) * coeff * (1.0 + 3.0 * 0.044715 * square)
        total[later, :] = slopes * total[later, :]
        total[now, :] = up * half
        return carry

    lax.fori_loop(0, ROWS // tile, activate, 0)
    for k in range(0, FF, 128):
        width = min(128, FF - k)
        hidden_v[pl.ds(k, width), :] = total[:, pl.ds(k, width)].T.astype(jnp.bfloat16)
    store = pltpu.make_async_copy(hidden_v, hidden, hidden_sem)
    store.start()
    finish_down(SENT_PARTS, parts, hidden_v, weight_v, part_v, down_sems, out_sems)
    store.wait()


def up_scratch(count):
    return (
        pltpu.VMEM((2 * ROWS, count * COLS), jnp.bfloat16),
        pltpu.VMEM((count * COLS, FF), jnp.bfloat16),
        pltpu.SemaphoreType.DMA((count,)),
        pltpu.SemaphoreType.DMA((count,)),
    )


def up_first(rows, arrays):
    return pl.pallas_call(
        up_first_kernel,
        in_specs=[pl.BlockSpec(memory_space=pl.ANY)] * 11,
        out_specs=pl.BlockSpec(memory_space=pltpu.VMEM),
        out_shape=jax.ShapeDtypeStruct((2 * ROWS, FF), jnp.float32),
        scratch_shapes=up_scratch(5),
        compiler_params=pltpu.CompilerParams(vmem_limit_bytes=VMEM_LIMIT),
        cost_estimate=pl.CostEstimate(flops=2 * ROWS * D * FF, bytes_accessed=9000000, transcendentals=0),
        name="up_first",
    )(rows, *arrays)


def down_scratch(parts):
    return (
        pltpu.VMEM((D, FF), jnp.bfloat16),
        pltpu.VMEM((D, 2 * ROWS), jnp.bfloat16),
        pltpu.SemaphoreType.DMA((16,)),
        pltpu.SemaphoreType.DMA((len(parts),)),
    )


def up_second(rows, before, arrays, last):
    shapes = [(FF, 2 * ROWS)] + [(columns, 2 * ROWS) for _, _, columns in SENT_PARTS]
    hidden, *parts = pl.pallas_call(
        up_second_kernel,
        in_specs=[pl.BlockSpec(memory_space=pl.ANY)] * 22,
        out_specs=[pl.BlockSpec(memory_space=pl.ANY)] * len(shapes),
        out_shape=[jax.ShapeDtypeStruct(shape, jnp.bfloat16) for shape in shapes],
        scratch_shapes=(
            pltpu.VMEM((FF, 2 * ROWS), jnp.bfloat16),
            pltpu.SemaphoreType.DMA,
            *down_scratch(SENT_PARTS),
            pltpu.VMEM((2 * ROWS, FF), jnp.float32),
            pltpu.SemaphoreType.DMA,
            *up_scratch(3),
        ),
        compiler_params=pltpu.CompilerParams(vmem_limit_bytes=VMEM_LIMIT),
        cost_estimate=pl.CostEstimate(flops=4 * ROWS * D * FF, bytes_accessed=14000000, transcendentals=ROWS * FF),
        name="up_second",
    )(rows, before, *arrays, *last)
    return hidden, parts


SENT_PARTS = ((7, 0, 320), (7, 320, 320), (5, 0, 640), (4, 0, 640))
KEPT_PARTS = (
    (6, 0, 320),
    (6, 320, 320),
    (1, 0, 640),
    (3, 0, 320),
    (3, 320, 320),
    (2, 0, 320),
    (2, 320, 320),
    (0, 0, 640),
)


def start_down(parts, arrays, weight_v, sems):
    swaps = [RING[k] for k in (1, 2, 3, 4)] + [SIDE[k] for k in (1, 2, 3, 4)]
    for array, block, _, spot, _ in ring_blocks(1, START, swaps):
        target = weight_v.at[pl.ds(pl.multiple_of(spot * WBLK, 32), WBLK), :]
        copy = pltpu.make_async_copy(arrays[array].at[block], target, sems.at[spot // 2])
        first = spot % 4 * WBLK
        here = [(spot // 4 == k) & (first >= start) & (first < start + columns) for k, start, columns in parts]
        pl.when(functools.reduce(lambda p, q: p | q, here))(copy.start)


def finish_down(parts, outs, hidden_v, weight_v, part_v, sems, out_sems):
    copies = []
    for n, (k, start, columns) in enumerate(parts):
        mine = pl.ds(k * COLS + start, columns)
        for first in range(start, start + columns, 2 * WBLK):
            two = weight_v.at[pl.ds(k * COLS + first, 2 * WBLK), :]
            pltpu.make_async_copy(two, two, sems.at[2 * k + first // (2 * WBLK)]).wait()
        part = jnp.dot(weight_v[mine, :], hidden_v[...], preferred_element_type=jnp.float32)
        part_v[mine, :] = part.astype(jnp.bfloat16)
        copies.append(pltpu.make_async_copy(part_v.at[mine, :], outs[n], out_sems.at[n]))
        copies[-1].start()
    for copy in copies:
        copy.wait()


def down_kernel(hidden, *refs):
    arrays, outs = refs[:18], refs[18 : 18 + len(KEPT_PARTS)]
    hidden_v, hidden_sem, weight_v, part_v, sems, out_sems = refs[18 + len(KEPT_PARTS) :]
    load = pltpu.make_async_copy(hidden, hidden_v, hidden_sem)
    load.start()
    start_down(KEPT_PARTS, arrays, weight_v, sems)
    load.wait()
    finish_down(KEPT_PARTS, outs, hidden_v, weight_v, part_v, sems, out_sems)


def down_product(hidden, arrays):
    return pl.pallas_call(
        down_kernel,
        in_specs=[pl.BlockSpec(memory_space=pl.ANY)] * (1 + len(arrays)),
        out_specs=[pl.BlockSpec(memory_space=pl.ANY)] * len(KEPT_PARTS),
        out_shape=[jax.ShapeDtypeStruct((columns, 2 * ROWS), jnp.bfloat16) for _, _, columns in KEPT_PARTS],
        scratch_shapes=(
            pltpu.VMEM((FF, 2 * ROWS), jnp.bfloat16),
            pltpu.SemaphoreType.DMA,
            *down_scratch(KEPT_PARTS),
        ),
        compiler_params=pltpu.CompilerParams(vmem_limit_bytes=VMEM_LIMIT),
        cost_estimate=pl.CostEstimate(flops=2 * ROWS * D * FF, bytes_accessed=8000000, transcendentals=0),
        name="down_product",
    )(hidden, *arrays)


def added(*terms):
    return sum(t.astype(jnp.float32) for t in terms).astype(jnp.bfloat16)


def out_kernel(kept, partner, down, down_early, up_early, up, mod, tmod, block_out, block_tangent):
    outgate = mod[...].astype(jnp.float32)[2:3]
    toutgate = tmod[...].astype(jnp.float32)[2:3]
    half = COLS // 2
    for k in range(0, COLS, 64):
        cols = pl.ds(k, 64)
        late = pl.ds(k % half, 64)
        sides = (down, up_early) if k < half else (down_early, up)
        terms = [kept[cols, :], partner[cols, :], sides[0][late, :], sides[1][late, :]]
        tile = sum(t.astype(jnp.float32) for t in terms)
        if k % 128 == 0:
            before = tile
            continue
        tile = jnp.concatenate([before, tile], 0).T
        cols = pl.ds(k - 64, 128)
        mixed = tile[:ROWS]
        gate = outgate[:, k - 64 : k + 64]
        tgate = toutgate[:, k - 64 : k + 64]
        block_out[:, cols] = (gate * mixed).astype(jnp.bfloat16)
        block_tangent[:, cols] = (tgate * mixed + gate * tile[ROWS:]).astype(jnp.bfloat16)


def gated(terms, modulation, mod_tangent):
    return pl.pallas_call(
        out_kernel,
        in_specs=[pl.BlockSpec(memory_space=pltpu.VMEM)] * 8,
        out_specs=[pl.BlockSpec(memory_space=pltpu.VMEM)] * 2,
        out_shape=[jax.ShapeDtypeStruct((ROWS, COLS), jnp.bfloat16)] * 2,
        compiler_params=pltpu.CompilerParams(vmem_limit_bytes=VMEM_LIMIT),
        cost_estimate=pl.CostEstimate(flops=10 * ROWS * COLS, bytes_accessed=3500000, transcendentals=0),
        name="gated",
    )(*terms, modulation, mod_tangent)


def shards(tokens, tangent, modulation, mod_tangent, up_weight, down_weight):
    own = packed(tokens, tangent, modulation, mod_tangent)
    mine = jnp.stack([down_weight.T, up_weight])

    other = core_swap(mine)
    far = y_far(up_weight)[None]
    from_low = x_up(own)
    from_high = x_down(own)
    near = y_near(after(own, far))
    m1 = z_ring(jnp.concatenate([other[1:], other[:1], mine], 0))
    far_other = core_swap(far)
    m1, far, far_other, from_low, from_high, near = fence(m1, far, far_other, from_low, from_high, near)

    near_low = x_up(near)
    near_high = x_down(near)
    m2 = z_ring(jnp.concatenate([m1, far, far_other], 0))
    s1 = core_swap(m1)
    q1 = y_far(after(jnp.concatenate([mine[:1], m1[1:3]], 0), s1))
    m2, s1, q1, near_low, near_high = fence(m2, s1, q1, near_low, near_high)

    across_low = x_up(jnp.concatenate([from_low[:ROWS], near_low[:ROWS]], 0))
    across_high = x_down(jnp.concatenate([from_high[ROWS:], near_high[ROWS:]], 0))
    m3 = z_ring(m2)
    q2 = y_far(m2[1:3])
    s2 = core_swap(m2)
    m3, s2, q2, across_low, across_high = fence(m3, s2, q2, across_low, across_high)

    m4 = z_ring(m3[2:])
    q3 = y_far(m3[1:3])
    s3 = core_swap(m3)
    t1 = core_swap(q1)
    rows = shape_rows([own, near, from_low, from_high, near_low, near_high], across_low, across_high)
    rows = rows.reshape(2 * ROWS, D)
    m4, q3, s3, t1, rows = fence(m4, q3, s3, t1, rows)

    m5 = z_ring(m4[2:3])
    q4 = y_far(m4[:1])
    s4 = core_swap(m4)
    t2 = core_swap(q2)
    start = [mine, other]
    total = up_first(rows, [*start, far, far_other, m1, s1, m2, s2, m3, s3])
    m5, s4, t2, q4, total = fence(m5, s4, t2, q4, total)

    s5 = core_swap(m5)
    t3 = core_swap(q3)
    t4 = core_swap(q4)
    s5, t3, t4, total = fence(s5, t3, t4, total)
    arrays = [*start, m1, s1, m2, s2, m3, s3, m4, s4, q1, t1, q2, t2, q3, t3, q4, t4]
    hidden, first = up_second(rows, total, arrays, [m5, s5])
    from_near = [y_near(first[0]), y_near(first[1])]
    near_from_low = x_up(first[2])
    near_from_high = x_down(first[3])
    rest = down_product(hidden, arrays)
    from_near[0], rest = lax.optimization_barrier((from_near[0], rest))
    far_up, far_down, partner, to_high, stay_high, stay_low, to_low, kept = rest
    from_far_low = x_up(added(far_up, from_near[0]))
    from_far_high = x_down(added(far_down, from_near[1]))
    from_partner = y_near(added(partner, near_from_low, near_from_high))
    from_down_early = x_up(after(stay_high, near_from_low))
    from_up_early = x_down(after(stay_low, near_from_high))
    from_down = x_up(added(to_high, from_far_low))
    from_up = x_down(added(to_low, from_far_high))
    terms = [kept, from_partner, from_down, from_down_early, from_up_early, from_up]
    block_out, block_tangent = gated(terms, modulation, mod_tangent)
    return (block_out, block_tangent)


def solution(mesh):
    return jax.shard_map(
        shards,
        mesh=mesh,
        in_specs=(
            P("ctx", "tp"),
            P("ctx", "tp"),
            P(None, "tp"),
            P(None, "tp"),
            P("ctx", "tp"),
            P("tp", "ctx"),
        ),
        out_specs=(P("ctx", "tp"), P("ctx", "tp")),
        check_vma=False,
    )
```

```python
import functools
import math

import jax
import jax.numpy as jnp
from jax import lax
from jax.experimental import pallas as pl
from jax.experimental.pallas import tpu as pltpu
from jax.sharding import PartitionSpec as P

D = 5120
ROWS = 256
COLS = 640
FF = 864
WBLK = 160
VMEM_LIMIT = 56 * 1024 * 1024


def ctx_perm(move):
    pairs = []
    for i in range(32):
        h, z, c = move(i // 16, (i // 2) % 8, i % 2)
        pairs.append((i, ((h % 2) * 8 + z % 8) * 2 + c % 2))
    return pairs


def tp_perm(move):
    pairs = []
    for i in range(8):
        x, y = move(i // 2, i % 2)
        pairs.append((i, (x % 4) * 2 + y % 2))
    return pairs


def x_up(v):
    return lax.ppermute(v, "tp", tp_perm(lambda x, y: (x + 1, y)))


def x_down(v):
    return lax.ppermute(v, "tp", tp_perm(lambda x, y: (x - 1, y)))


def y_near(v):
    return lax.ppermute(v, "tp", tp_perm(lambda x, y: (x, y + 1)))


def y_far(v):
    return lax.ppermute(v, "ctx", ctx_perm(lambda h, z, c: (h + 1, z, c)))


def core_swap(v):
    return lax.ppermute(v, "ctx", ctx_perm(lambda h, z, c: (h, z, c + 1)))


def z_ring(v):
    return lax.ppermute(v, "ctx", ctx_perm(lambda h, z, c: (h, z + 1 - 2 * c, c)))


def place():
    t = lax.axis_index("tp")
    i = lax.axis_index("ctx")
    return t // 2, t % 2, i // 16, (i // 2) % 8, i % 2


def near_order(x, y, h, z):
    owner = h * 4 + z // 2
    dx = (owner // 2 - x + 4) % 4
    dy = (owner % 2 - y + 2) % 2
    side = jnp.where(dx == 3, 2, 3) + 2 * dy
    return jnp.where(dx == 0, dy, jnp.where(dx == 2, 6 + dy, side))


def after(value, *others):
    return lax.optimization_barrier((value, *others))[0]


def fence(*values):
    return lax.optimization_barrier(values)


START = tuple(((1, 0, 0, own), (0, 0, 0, own)) for own in (1, 0))
FAR_START = tuple(((0, 1, 0, own),) for own in (1, 0))


def ring_step(step):
    blocks = ((0, 0, step, 0), (1, 0, step, 0), (1, 0, step, 1), (0, 0, step, 1))
    if step > 1:
        blocks += ((0, 1, step - 1, 1), (0, 1, step - 1, 0))
    return blocks


RING = {k: ring_step(k) for k in (1, 2, 3)}
RING[4] = ((1, 0, 4, 1), (0, 0, 4, 1), (0, 1, 3, 1), (0, 1, 3, 0))
RING[5] = ((0, 1, 4, 1),)
SIDE = {k: ((1, 1, k, 0), (1, 1, k, 1)) for k in (1, 2, 3)}
SIDE[1] = ((1, 1, 0, 1), *SIDE[1])
SIDE[4] = ((1, 1, 4, 1),)


def ring_blocks(kind, sources, swaps):
    x, y, h, z, c = place()
    out = []
    arrays = [(blocks, False) for blocks in sources]
    for blocks in swaps:
        arrays += [(blocks, False), (blocks, True)]
    for array, (blocks, swapped) in enumerate(arrays):
        for block, (of, stream, step, own) in enumerate(blocks):
            if of != kind:
                continue
            sign = 1 - 2 * c
            there = (z + (step * sign if swapped else -step * sign) + 8) % 8
            core = c if bool(own) != swapped else 1 - c
            spot = near_order(x, y, 1 - h if stream else h, there) * 4 + (there % 2) * 2 + core
            out.append((array, block, stream, spot, there // 2))
    return out


def pack_kernel(tokens, tangent, modulation, mod_tangent, out):
    out[:ROWS, :] = tokens[...]
    out[ROWS : 2 * ROWS, :] = tangent[...]
    mods = [modulation[...].astype(jnp.float32), mod_tangent[...].astype(jnp.float32)]
    tail = jnp.concatenate([*mods, jnp.zeros((10, COLS), jnp.float32)], 0)
    out[2 * ROWS :, :] = tail.astype(jnp.bfloat16)


def packed(*arrays):
    return pl.pallas_call(
        pack_kernel,
        in_specs=[pl.BlockSpec(memory_space=pltpu.VMEM)] * 4,
        out_specs=pl.BlockSpec(memory_space=pltpu.VMEM),
        out_shape=jax.ShapeDtypeStruct((2 * ROWS + 16, COLS), jnp.bfloat16),
        cost_estimate=pl.CostEstimate(flops=10**11, bytes_accessed=1400000, transcendentals=0),
        name="packed",
    )(*arrays)


def shape_kernel(*refs):
    whole, across_low, across_high, out = refs[:6], refs[6], refs[7], refs[8]
    toks = [(r, 0) for r in whole] + [(across_low, 0), (across_low, ROWS)]
    tans = [(r, ROWS) for r in whole] + [(across_high, 0), (across_high, ROWS + 16)]
    spread = refs[9]
    lanes = [(k, pl.ds(n, 128), k * COLS + n) for k in range(8) for n in range(0, COLS, 128)]
    tile = out.shape[1]

    @pl.when(pl.program_id(0) == 0)
    def _():
        for k, cols, first in lanes:
            ref, base = tans[k]
            mod = ref[pl.ds(base + ROWS, 16), cols].astype(jnp.float32)
            for n, row in enumerate((mod[0:1], 1.0 + mod[1:2], mod[3:4], mod[4:5])):
                spread[n, :, pl.ds(first, 128)] = jnp.broadcast_to(row, (16, 128))

    start = pl.program_id(0) * tile

    def load(source, k, cols, first):
        ref, base = source[k]
        return ref[pl.ds(pl.multiple_of(base + first, 16), 16), cols].astype(jnp.float32)

    def sixteen(i, carry):
        first = start + i * 16
        sums = [jnp.zeros((16, 128), jnp.float32) for _ in range(4)]
        for k, cols, _ in lanes:
            t = load(toks, k, cols, first)
            u = load(tans, k, cols, first)
            sums = [sums[0] + t, sums[1] + t * t, sums[2] + u, sums[3] + t * u]
        row_sum, square_sum, tan_sum, cross_sum = [jnp.sum(p, axis=1, keepdims=True) for p in sums]
        row_mean = row_sum / D
        inverse_std = lax.rsqrt(square_sum / D - row_mean * row_mean + 1e-06)
        tan_mean = tan_sum / D
        crossed = (cross_sum / D - row_mean * tan_mean) * inverse_std
        back = crossed * inverse_std
        rows = pl.ds(pl.multiple_of(i * 16, 16), 16)
        for k, cols, place_of in lanes:
            target = pl.ds(place_of, 128)
            shift, gain, tshift, tscale = (spread[n, :, target] for n in range(4))
            normed = (load(toks, k, cols, first) - row_mean) * inverse_std
            tnormed = (load(tans, k, cols, first) - tan_mean) * inverse_std - normed * back
            out[0, rows, target] = (normed * gain + shift).astype(jnp.bfloat16)
            out[1, rows, target] = (tnormed * gain + normed * tscale + tshift).astype(jnp.bfloat16)
        return carry

    lax.fori_loop(0, tile // 16, sixteen, 0)


def shape_rows(whole, across_low, across_high):
    tile = 64
    sources = [*whole, across_low, across_high]
    return pl.pallas_call(
        shape_kernel,
        grid=(ROWS // tile,),
        in_specs=[pl.BlockSpec(a.shape, lambda i: (0, 0)) for a in sources],
        out_specs=pl.BlockSpec((2, tile, D), lambda i: (0, i, 0)),
        out_shape=jax.ShapeDtypeStruct((2, ROWS, D), jnp.bfloat16),
        scratch_shapes=[pltpu.VMEM((4, 16, D), jnp.float32)],
        compiler_params=pltpu.CompilerParams(vmem_limit_bytes=VMEM_LIMIT),
        cost_estimate=pl.CostEstimate(flops=30 * ROWS * D, bytes_accessed=8 * ROWS * D, transcendentals=0),
        name="shape_rows",
    )(*sources)


def feature_products(rows, arrays, blocks, wanted, groups, rows_v, weight_v, row_sems, weight_sems):
    x, y, h, _, _ = place()
    order = [near_order(x, y, 1 - h if stream else h, 2 * pair) for stream, pair in wanted]

    def row_copy(n):
        cols = pl.ds(pl.multiple_of(order[n] * COLS, 128), COLS)
        return pltpu.make_async_copy(rows.at[:, cols], rows_v.at[:, pl.ds(n * COLS, COLS)], row_sems.at[n])

    for n in range(len(order)):
        row_copy(n).start()
    for array, block, stream, spot, pair in blocks:
        here = [(n, pair == other) for n, (of, other) in enumerate(wanted) if of == stream]
        slot = sum(jnp.where(same, n, 0) for n, same in here)
        target = weight_v.at[pl.ds(pl.multiple_of(slot * COLS + spot % 4 * WBLK, 32), WBLK), :]
        copy = pltpu.make_async_copy(arrays[array].at[block], target, weight_sems.at[slot])
        pl.when(functools.reduce(lambda p, q: p | q, [same for _, same in here]))(copy.start)
    yield None
    first = 0
    for group in groups:
        for n in range(first, first + group):
            row_copy(n).wait()
            block = weight_v.at[pl.ds(n * COLS, COLS), :]
            pltpu.make_async_copy(block, block, weight_sems.at[n]).wait()
        span = pl.ds(first * COLS, group * COLS)
        yield jnp.dot(rows_v[:, span], weight_v[span, :], preferred_element_type=jnp.float32)
        first += group


def pair_order():
    z = place()[3]
    side = 2 * (z % 2) - 1
    return [z // 2, (z // 2 + side + 4) % 4, (z // 2 - side + 4) % 4, (z // 2 + 2) % 4]


def up_first_kernel(rows, *refs):
    arrays, total, scratch = refs[:10], refs[10], refs[11:]
    p = pair_order()
    wanted = [(0, p[0]), (0, p[1]), (1, p[0]), (0, p[2]), (1, p[1])]
    blocks = ring_blocks(0, START + FAR_START, [RING[k] for k in (1, 2, 3)])
    _, first, second = feature_products(rows, arrays, blocks, wanted, (3, 2), *scratch)
    total[...] = first
    total[...] += second


def up_second_kernel(rows, before, *refs):
    arrays, last, hidden, parts = refs[:18], refs[18:20], refs[20], refs[21:25]
    hidden_v, hidden_sem, weight_v, part_v, down_sems, out_sems, total, before_sem = refs[25:33]
    p = pair_order()
    wanted = [(1, p[2]), (0, p[3]), (1, p[3])]
    blocks = ring_blocks(0, (), [RING[k] for k in (3, 4, 5)])
    products = feature_products(rows, [*arrays[6:10], *last], blocks, wanted, (3,), *refs[33:])
    next(products)
    load = pltpu.make_async_copy(before, total, before_sem)
    load.start()
    start_down(SENT_PARTS, arrays, weight_v, down_sems)
    (part,) = products
    load.wait()
    total[...] += part
    coeff = math.sqrt(2.0 / math.pi)
    tile = 16

    def activate(k, carry):
        now = pl.ds(pl.multiple_of(k * tile, tile), tile)
        later = pl.ds(pl.multiple_of(ROWS + k * tile, tile), tile)
        up = total[now, :]
        square = up * up
        th = jnp.tanh(coeff * (up + 0.044715 * up * square))
        half = 0.5 * (1.0 + th)
        slopes = half + 0.5 * up * (1.0 - th * th) * coeff * (1.0 + 3.0 * 0.044715 * square)
        total[later, :] = slopes * total[later, :]
        total[now, :] = up * half
        return carry

    lax.fori_loop(0, ROWS // tile, activate, 0)
    for k in range(0, FF, 128):
        width = min(128, FF - k)
        hidden_v[pl.ds(k, width), :] = total[:, pl.ds(k, width)].T.astype(jnp.bfloat16)
    store = pltpu.make_async_copy(hidden_v, hidden, hidden_sem)
    store.start()
    finish_down(SENT_PARTS, parts, hidden_v, weight_v, part_v, down_sems, out_sems)
    store.wait()


def up_scratch(count):
    return (
        pltpu.VMEM((2 * ROWS, count * COLS), jnp.bfloat16),
        pltpu.VMEM((count * COLS, FF), jnp.bfloat16),
        pltpu.SemaphoreType.DMA((count,)),
        pltpu.SemaphoreType.DMA((count,)),
    )


def up_first(rows, arrays):
    return pl.pallas_call(
        up_first_kernel,
        in_specs=[pl.BlockSpec(memory_space=pl.ANY)] * 11,
        out_specs=pl.BlockSpec(memory_space=pltpu.VMEM),
        out_shape=jax.ShapeDtypeStruct((2 * ROWS, FF), jnp.float32),
        scratch_shapes=up_scratch(5),
        compiler_params=pltpu.CompilerParams(vmem_limit_bytes=VMEM_LIMIT),
        cost_estimate=pl.CostEstimate(flops=2 * ROWS * D * FF, bytes_accessed=9000000, transcendentals=0),
        name="up_first",
    )(rows, *arrays)


def down_scratch(parts):
    return (
        pltpu.VMEM((D, FF), jnp.bfloat16),
        pltpu.VMEM((D, 2 * ROWS), jnp.bfloat16),
        pltpu.SemaphoreType.DMA((16,)),
        pltpu.SemaphoreType.DMA((len(parts),)),
    )


def up_second(rows, before, arrays, last):
    shapes = [(FF, 2 * ROWS)] + [(columns, 2 * ROWS) for _, _, columns in SENT_PARTS]
    hidden, *parts = pl.pallas_call(
        up_second_kernel,
        in_specs=[pl.BlockSpec(memory_space=pl.ANY)] * 22,
        out_specs=[pl.BlockSpec(memory_space=pl.ANY)] * len(shapes),
        out_shape=[jax.ShapeDtypeStruct(shape, jnp.bfloat16) for shape in shapes],
        scratch_shapes=(
            pltpu.VMEM((FF, 2 * ROWS), jnp.bfloat16),
            pltpu.SemaphoreType.DMA,
            *down_scratch(SENT_PARTS),
            pltpu.VMEM((2 * ROWS, FF), jnp.float32),
            pltpu.SemaphoreType.DMA,
            *up_scratch(3),
        ),
        compiler_params=pltpu.CompilerParams(vmem_limit_bytes=VMEM_LIMIT),
        cost_estimate=pl.CostEstimate(flops=4 * ROWS * D * FF, bytes_accessed=14000000, transcendentals=ROWS * FF),
        name="up_second",
    )(rows, before, *arrays, *last)
    return hidden, parts


SENT_PARTS = ((7, 0, 320), (7, 320, 320), (5, 0, 640), (4, 0, 640))
FAR_PARTS = ((6, 0, 320), (6, 320, 320), (1, 0, 640))
KEPT_PARTS = ((3, 0, 320), (3, 320, 320), (2, 0, 320), (2, 320, 320), (0, 0, 640))


def start_down(parts, arrays, weight_v, sems):
    swaps = [RING[k] for k in (1, 2, 3, 4)] + [SIDE[k] for k in (1, 2, 3, 4)]
    for array, block, _, spot, _ in ring_blocks(1, START, swaps):
        target = weight_v.at[pl.ds(pl.multiple_of(spot * WBLK, 32), WBLK), :]
        copy = pltpu.make_async_copy(arrays[array].at[block], target, sems.at[spot // 2])
        first = spot % 4 * WBLK
        here = [(spot // 4 == k) & (first >= start) & (first < start + columns) for k, start, columns in parts]
        pl.when(functools.reduce(lambda p, q: p | q, here))(copy.start)


def finish_down(parts, outs, hidden_v, weight_v, part_v, sems, out_sems):
    copies = []
    for n, (k, start, columns) in enumerate(parts):
        mine = pl.ds(k * COLS + start, columns)
        for first in range(start, start + columns, 2 * WBLK):
            two = weight_v.at[pl.ds(k * COLS + first, 2 * WBLK), :]
            pltpu.make_async_copy(two, two, sems.at[2 * k + first // (2 * WBLK)]).wait()
        part = jnp.dot(weight_v[mine, :], hidden_v[...], preferred_element_type=jnp.float32)
        part_v[mine, :] = part.astype(jnp.bfloat16)
        copies.append(pltpu.make_async_copy(part_v.at[mine, :], outs[n], out_sems.at[n]))
        copies[-1].start()
    for copy in copies:
        copy.wait()


def down_kernel(parts, hidden, *refs):
    arrays, outs = refs[:18], refs[18 : 18 + len(parts)]
    hidden_v, hidden_sem, weight_v, part_v, sems, out_sems = refs[18 + len(parts) :]
    load = pltpu.make_async_copy(hidden, hidden_v, hidden_sem)
    load.start()
    start_down(parts, arrays, weight_v, sems)
    load.wait()
    finish_down(parts, outs, hidden_v, weight_v, part_v, sems, out_sems)


def down_product(hidden, arrays, parts):
    return pl.pallas_call(
        functools.partial(down_kernel, parts),
        in_specs=[pl.BlockSpec(memory_space=pl.ANY)] * (1 + len(arrays)),
        out_specs=[pl.BlockSpec(memory_space=pl.ANY)] * len(parts),
        out_shape=[jax.ShapeDtypeStruct((columns, 2 * ROWS), jnp.bfloat16) for _, _, columns in parts],
        scratch_shapes=(
            pltpu.VMEM((FF, 2 * ROWS), jnp.bfloat16),
            pltpu.SemaphoreType.DMA,
            *down_scratch(parts),
        ),
        compiler_params=pltpu.CompilerParams(vmem_limit_bytes=VMEM_LIMIT),
        cost_estimate=pl.CostEstimate(flops=2 * ROWS * D * FF, bytes_accessed=8000000, transcendentals=0),
        name="down_product",
    )(hidden, *arrays)


def added(*terms):
    return sum(t.astype(jnp.float32) for t in terms).astype(jnp.bfloat16)


def out_kernel(kept, partner, down, down_early, up_early, up, mod, tmod, block_out, block_tangent):
    outgate = mod[...].astype(jnp.float32)[2:3]
    toutgate = tmod[...].astype(jnp.float32)[2:3]
    half = COLS // 2
    for k in range(0, COLS, 64):
        cols = pl.ds(k, 64)
        late = pl.ds(k % half, 64)
        sides = (down, up_early) if k < half else (down_early, up)
        terms = [kept[cols, :], partner[cols, :], sides[0][late, :], sides[1][late, :]]
        tile = sum(t.astype(jnp.float32) for t in terms)
        if k % 128 == 0:
            before = tile
            continue
        tile = jnp.concatenate([before, tile], 0).T
        cols = pl.ds(k - 64, 128)
        mixed = tile[:ROWS]
        gate = outgate[:, k - 64 : k + 64]
        tgate = toutgate[:, k - 64 : k + 64]
        block_out[:, cols] = (gate * mixed).astype(jnp.bfloat16)
        block_tangent[:, cols] = (tgate * mixed + gate * tile[ROWS:]).astype(jnp.bfloat16)


def gated(terms, modulation, mod_tangent):
    return pl.pallas_call(
        out_kernel,
        in_specs=[pl.BlockSpec(memory_space=pltpu.VMEM)] * 8,
        out_specs=[pl.BlockSpec(memory_space=pltpu.VMEM)] * 2,
        out_shape=[jax.ShapeDtypeStruct((ROWS, COLS), jnp.bfloat16)] * 2,
        compiler_params=pltpu.CompilerParams(vmem_limit_bytes=VMEM_LIMIT),
        cost_estimate=pl.CostEstimate(flops=10 * ROWS * COLS, bytes_accessed=3500000, transcendentals=0),
        name="gated",
    )(*terms, modulation, mod_tangent)


def shards(tokens, tangent, modulation, mod_tangent, up_weight, down_weight):
    own = packed(tokens, tangent, modulation, mod_tangent)
    mine = jnp.stack([down_weight.T, up_weight])

    other = core_swap(mine)
    far = y_far(up_weight)[None]
    from_low = x_up(own)
    from_high = x_down(own)
    near = y_near(after(own, far))
    m1 = z_ring(jnp.concatenate([other[1:], other[:1], mine], 0))
    far_other = core_swap(far)
    m1, far, far_other, from_low, from_high, near = fence(m1, far, far_other, from_low, from_high, near)

    near_low = x_up(near)
    near_high = x_down(near)
    m2 = z_ring(jnp.concatenate([m1, far, far_other], 0))
    s1 = core_swap(m1)
    q1 = y_far(after(jnp.concatenate([mine[:1], m1[1:3]], 0), s1))
    m2, s1, q1, near_low, near_high = fence(m2, s1, q1, near_low, near_high)

    across_low = x_up(jnp.concatenate([from_low[:ROWS], near_low[:ROWS]], 0))
    across_high = x_down(jnp.concatenate([from_high[ROWS:], near_high[ROWS:]], 0))
    m3 = z_ring(m2)
    q2 = y_far(m2[1:3])
    s2 = core_swap(m2)
    m3, s2, q2, across_low, across_high = fence(m3, s2, q2, across_low, across_high)

    m4 = z_ring(m3[2:])
    q3 = y_far(m3[1:3])
    s3 = core_swap(m3)
    t1 = core_swap(q1)
    rows = shape_rows([own, near, from_low, from_high, near_low, near_high], across_low, across_high)
    rows = rows.reshape(2 * ROWS, D)
    m4, q3, s3, t1, rows = fence(m4, q3, s3, t1, rows)

    m5 = z_ring(m4[2:3])
    q4 = y_far(m4[:1])
    s4 = core_swap(m4)
    t2 = core_swap(q2)
    start = [mine, other]
    total = up_first(rows, [*start, far, far_other, m1, s1, m2, s2, m3, s3])
    m5, s4, t2, q4, total = fence(m5, s4, t2, q4, total)

    s5 = core_swap(m5)
    t3 = core_swap(q3)
    t4 = core_swap(q4)
    s5, t3, t4, total = fence(s5, t3, t4, total)
    arrays = [*start, m1, s1, m2, s2, m3, s3, m4, s4, q1, t1, q2, t2, q3, t3, q4, t4]
    hidden, first = up_second(rows, total, arrays, [m5, s5])
    from_near = [y_near(first[0]), y_near(first[1])]
    near_from_low = x_up(first[2])
    near_from_high = x_down(first[3])
    far_up, far_down, partner = down_product(hidden, arrays, FAR_PARTS)
    far_sum = added(far_up, from_near[0])
    from_far_low = x_up(far_sum)
    to_high, stay_high, stay_low, to_low, kept = down_product(after(hidden, far_sum), arrays, KEPT_PARTS)
    from_far_high = x_down(added(far_down, from_near[1]))
    from_partner = y_near(added(partner, near_from_low, near_from_high))
    from_down_early = x_up(after(stay_high, near_from_low))
    from_up_early = x_down(after(stay_low, near_from_high))
    from_down = x_up(added(to_high, from_far_low))
    from_up = x_down(added(to_low, from_far_high))
    terms = [kept, from_partner, from_down, from_down_early, from_up_early, from_up]
    block_out, block_tangent = gated(terms, modulation, mod_tangent)
    return (block_out, block_tangent)


def solution(mesh):
    return jax.shard_map(
        shards,
        mesh=mesh,
        in_specs=(
            P("ctx", "tp"),
            P("ctx", "tp"),
            P(None, "tp"),
            P(None, "tp"),
            P("ctx", "tp"),
            P("tp", "ctx"),
        ),
        out_specs=(P("ctx", "tp"), P("ctx", "tp")),
        check_vma=False,
    )
```
